32 devices in a mesh: leaf: 16 (over z, y, x), face: 2 (over core).
Axes of the slice: x: 2, y: 2, z: 4, core: 2. Of those that a mesh axis runs over, the one named last changes fastest.
Arguments:
- solve_ops: bfloat16 [32, 216, 384], P('leaf'), may hold values from -0.30618622 to 0.30618622, as said below
- inner_deriv: bfloat16 [6, 2, 32, 216], P(None, 'face'), may hold values from -1.796875 to 1.796875
- boundary_diag: float32 [6, 2, 32], P(None, 'face'), may hold values from 2.5 to 5
- wall_stencil: float32 [2, 32, 64], P('face'), may hold values from -0.3 to 0.3
- wall_coef: float32 [32, 6], P('leaf'), may hold values from 0.5 to 4
- cut_faces: int32 [32, 6], P('leaf'), may hold values 0 or 1
Outputs:
- merged: float32 [32, 4, 2, 32, 1024], P('leaf', None, 'face')
The draws below stay inside these ranges and needn't reach their ends.
Inputs may be any that keep to these rules, and one draw needn't show every extreme that they name: `solve_ops`: entries of spread about 384 to the power -1/2.
All inputs are finite; a program needn't handle non-finite values. No bound on the sum of `cut_faces` on one device may be relied on, other than what follows from the above.
Results may differ from the reference program's by a relative error of at most 0.0003.
Values sent between devices are 32-bit elements; how exact they have to be, the bound alone decides.
A program may use at most 64 MiB of HBM per device.

```python
import math
import jax
import jax.numpy as jnp
import numpy as np
from jax import lax

FP = 64
IN = 216
FACES = 6
LEAF_DEV = 2
HALF = 32
BP = 384
E2 = 1024
LEAVES = 32
N_LEAF = 16


def draw_solve_ops(key, part):
    key = jax.random.fold_in(key, 11)
    first_key = jax.random.fold_in(key, 0)
    values = jax.random.truncated_normal(first_key, -6.0, 6.0, (LEAVES, IN, BP), jnp.float32)
    return (values * BP ** (-0.5)).astype(jnp.bfloat16)


def plant(array, stream_key, least, top_value):
    shape = array.shape
    spot = [jax.random.randint(jax.random.fold_in(stream_key, axis), (), 0, shape[axis]) for axis in range(len(shape))]
    array = array.at[tuple(spot)].set(least)
    longest = shape.index(max(shape))
    spot[longest] = (spot[longest] + 1) % shape[longest]
    return array.at[tuple(spot)].set(top_value)


def level_of(own_key, shape, shards, low, top_value):
    gain = 1.0
    for position, blocks in shards:
        steps = jax.random.uniform(jax.random.fold_in(jax.random.fold_in(own_key, 6), position), (blocks,), jnp.float32, low / len(shards), top_value / len(shards))
        gain = gain * jnp.repeat(jnp.exp(steps), shape[position] // blocks).reshape((-1,) + (1,) * (len(shape) - 1 - position))
    return gain


def gaussian(stream_key, extent, scale, limit, pieces=(), held_as=jnp.bfloat16):
    drawn = jax.random.normal(stream_key, extent, jnp.float32) * scale
    if len(pieces) > 0:
        drawn = level_of(stream_key, extent, pieces, -0.22, 0.18) * drawn
    return jnp.clip(drawn, min=-limit, max=limit).astype(held_as)


def setup_inputs(seed: int = 0) -> dict:
    key_list = jax.random.split(jax.random.key(seed), 7)
    return {
        "solve_ops": draw_solve_ops(jax.random.fold_in(key_list[6], 71), 0),
        "inner_deriv": gaussian(key_list[1], (FACES, 2, HALF, IN), 0.3, 1.796875, ((1, 2),)),
        "boundary_diag": jnp.clip(2.5 + 2.5 * jax.random.uniform(key_list[2], (FACES, 2, HALF), jnp.float32) ** level_of(key_list[2], (FACES, 2, HALF), ((1, 2),), -0.2, 0.2), 2.5, 5.0),
        "wall_stencil": gaussian(key_list[3], (2, HALF, FP), 0.05, 0.3, ((0, 2),), jnp.float32),
        "wall_coef": jnp.clip(jnp.exp(math.log(4.0) - 2.0794415 * jax.random.uniform(key_list[4], (LEAVES, FACES), jnp.float32) ** level_of(key_list[4], (LEAVES, FACES), ((0, 16),), -0.2, 0.2)), 0.5, 4.0),
        "cut_faces": plant((jax.random.randint(key_list[5], (LEAVES, FACES), 0, 3) < 1).astype(jnp.int32), jax.random.fold_in(key_list[5], 1), 0, 1),
    }


def points(blocks, width):
    return np.concatenate([np.arange(width) + width * index for index in blocks]).astype(np.int32)

def merge_pair(left, right, inner_left, inner_right, outer_left, outer_right):
    left_inner = left[:, inner_left]
    right_inner = right[:, inner_right]
    schur = left_inner[:, :, inner_left] + right_inner[:, :, inner_right]
    coupled = jnp.concatenate([left_inner[:, :, outer_left], right_inner[:, :, outer_right]], axis=2)
    solved = jnp.linalg.solve(schur, coupled)
    count = left.shape[0]
    size_left = outer_left.shape[0]
    size_right = outer_right.shape[0]
    upper = jnp.concatenate([left[:, outer_left][:, :, outer_left], jnp.zeros((count, size_left, size_right), jnp.float32)], axis=2)
    lower = jnp.concatenate([jnp.zeros((count, size_right, size_left), jnp.float32), right[:, outer_right][:, :, outer_right]], axis=2)
    blocks = jnp.concatenate([upper, lower], axis=1)
    faces = jnp.concatenate([left[:, outer_left][:, :, inner_left], right[:, outer_right][:, :, inner_right]], axis=1)
    return blocks - jnp.matmul(faces, solved, precision=lax.Precision.HIGHEST)

def reference(solve_ops, inner_deriv, boundary_diag, wall_stencil, wall_coef, cut_faces):
    groups = N_LEAF // 4
    rows = inner_deriv.reshape(BP, IN).astype(jnp.float32)
    diagonal = jnp.diag(boundary_diag.reshape(BP).astype(jnp.float32))
    stencil = wall_stencil.reshape(FP, FP)
    same_face = jnp.eye(FACES, dtype=jnp.float32)

    def one_group(items):
        operators, strength, cut = items
        dtn = jnp.einsum('ri,dlic->dlrc', rows, operators.astype(jnp.float32), precision=lax.Precision.HIGHEST)
        dtn = dtn + diagonal
        weights = cut.astype(jnp.float32) * strength
        dtn = dtn + jnp.einsum('dlf,fg,pk->dlfpgk', weights, same_face, stencil).reshape(4, LEAF_DEV, BP, BP)
        pairs = []
        for box in range(2):
            pairs.append(merge_pair(dtn[2 * box], dtn[2 * box + 1], points([1], FP), points([0], FP), points([0, 2, 3, 4, 5], FP), points([1, 2, 3, 4, 5], FP)))
        quartet = merge_pair(pairs[0], pairs[1], points([2, 7], FP), points([1, 6], FP), points([0, 1, 3, 4, 5, 6, 8, 9], FP), points([0, 2, 3, 4, 5, 7, 8, 9], FP))
        quartet = quartet.reshape(LEAF_DEV, 2, 2, 4, 2, HALF, E2)
        return jnp.transpose(quartet, (1, 2, 0, 3, 4, 5, 6)).reshape(4 * LEAF_DEV, 4, 2, HALF, E2)
    result = lax.map(one_group, (solve_ops.reshape(groups, 4, LEAF_DEV, IN, BP), wall_coef.reshape(groups, 4, LEAF_DEV, FACES), cut_faces.reshape(groups, 4, LEAF_DEV, FACES)))
    return result.reshape(LEAVES, 4, 2, HALF, E2)
```

```python
import functools

import jax
import jax.numpy as jnp
from jax import lax
from jax.experimental import pallas as pl
from jax.experimental.pallas import tpu as pltpu
from jax.sharding import PartitionSpec as P

MESH = pl.DeviceIdType.MESH
F32 = jnp.float32
BF16 = jnp.bfloat16
LIMIT = 60


def lanes_of(shape):
    return lax.broadcasted_iota(jnp.int32, shape, len(shape) - 1)


def turn(x):
    return pltpu.roll(x, 64, 1)


def leaf_rows(values, diag, stencil, weights, faces, core, s, q):
    half = 32
    lane = lanes_of((half, 128))
    row = lax.broadcasted_iota(jnp.int32, (half, 128), 0)
    tiles = []
    for n, face in enumerate(faces):
        part = values[n * half : (n + 1) * half]
        side = face % 2
        spot = lane - side * 64
        extra = jnp.where(spot == core * half + row, diag[n], 0.0)
        on = jnp.logical_and(spot >= 0, spot < 64)
        extra = extra + jnp.where(on, stencil * weights[n], 0.0)
        tiles.append(
            [part[:, t * 128 : t * 128 + 128] + jnp.where(face // 2 == t, extra, 0.0) for t in range(3)]
        )
    xt, yt, zt = (jnp.concatenate([row_tiles[t] for row_tiles in tiles], axis=0) for t in range(3))
    left = lanes_of(xt.shape) < 64
    xr, yr = turn(xt), turn(yt)
    first, lower = s == 0, q == 0
    outer = jnp.where(left, jnp.where(first, xt, xr), jnp.where(lower, yr, yt))
    inner = jnp.where(left, jnp.where(first, xr, xt), jnp.where(lower, yt, yr))
    return outer, zt, inner


def gather_kernel(solve, deriv, diag, stencil, coef, cut, g, own, send, recv):
    me = lax.axis_index("leaf")
    core = lax.axis_index("face")
    s, q = me % 2, me // 2 % 2
    xdev = (me + 1 - 2 * s, core)
    ydev = (me + 2 - 4 * q, core)
    cdev = (me, 1 - core)
    barrier = pltpu.get_barrier_semaphore()
    for dev in (xdev, ydev, cdev):
        pl.semaphore_signal(barrier, inc=1, device_id=dev, device_id_type=MESH)

    rows = pl.ds(pl.multiple_of(core * 32, 32), 32)

    def copy(index, qq, ss, l, dev):
        where = g.at[qq, ss, l, :, rows, :]
        return pltpu.make_async_remote_copy(
            src_ref=where, dst_ref=where, send_sem=send.at[index], recv_sem=recv.at[index],
            device_id=dev, device_id_type=MESH,
        )

    st = stencil[0]
    st = jnp.concatenate([st, st], axis=1)

    def compute(l, faces):
        d = jnp.concatenate([deriv[f, 0] for f in faces], axis=0)
        values = jnp.dot(d, solve[l], preferred_element_type=F32)
        dd = [jnp.concatenate([diag[f]] * 4, axis=1) for f in faces]
        w = [cut[l, f].astype(F32) * coef[l, f] for f in faces]
        return leaf_rows(values, dd, st, w, faces, core, s, q)

    shared = (1 - s, 3 - q)
    for l in range(2):
        for t, tile in enumerate(compute(l, shared)):
            g[q, s, l, 0, rows, t * 128 : t * 128 + 128] = tile[:32]
            g[q, s, l, 1, rows, t * 128 : t * 128 + 128] = tile[32:]
    pl.semaphore_wait(barrier, 3)
    x0, y1 = copy(0, q, s, 0, xdev), copy(1, q, s, 1, ydev)
    x1, y0 = copy(2, q, s, 1, xdev), copy(3, q, s, 0, ydev)
    c0, c1 = copy(4, q, s, 0, cdev), copy(5, q, s, 1, cdev)
    started = [x0, y1, x1, y0, c0, c1]
    for one in started:
        one.start()
    kept = (s, 2 + q, 4, 5)
    for l in range(2):
        for t, tile in enumerate(compute(l, kept)):
            own[l, :, t * 128 : t * 128 + 128] = tile
    later = [
        (x0, [(6, q, 1 - s, 0, ydev), (7, q, 1 - s, 0, cdev)]),
        (y1, [(8, 1 - q, s, 1, xdev), (9, 1 - q, s, 1, cdev)]),
        (x1, [(10, q, 1 - s, 1, cdev)]),
        (y0, [(11, 1 - q, s, 0, cdev)]),
    ]
    done = {}
    for first, relays in later:
        first.wait_recv()
        for relay in relays:
            done[relay[0]] = copy(*relay)
            done[relay[0]].start()
    done[6].wait_recv()
    done[12] = copy(12, 1 - q, 1 - s, 0, cdev)
    done[12].start()
    done[8].wait_recv()
    done[13] = copy(13, 1 - q, 1 - s, 1, cdev)
    done[13].start()
    c0.wait_recv()
    c1.wait_recv()
    for index in (7, 9, 10, 11, 12, 13):
        done[index].wait_recv()
    for one in started + list(done.values()):
        one.wait_send()


def split(x):
    hi = x.astype(BF16)
    return hi, (x - hi.astype(F32)).astype(BF16)


def dot(a, b):
    return jnp.dot(a, b, preferred_element_type=F32)


def mul(a, b):
    ah, al = split(a)
    bh, bl = split(b)
    both = jnp.concatenate([ah, al], axis=1)
    if b.shape[1] == 128:
        weights = jnp.concatenate(
            [jnp.concatenate([bh, bl], axis=1), jnp.concatenate([bh, jnp.zeros_like(bl)], axis=1)], axis=0
        )
        out = dot(both, weights)
        return out[:, :128] + out[:, 128:]
    return dot(both, jnp.concatenate([bh, bh], axis=0)) + dot(ah, bl)


def invert(mats):
    row = lax.broadcasted_iota(jnp.int32, (128, 128), 0)
    eye = (row == lanes_of((128, 128))).astype(F32)
    state = []
    for m in mats:
        mt = m.T
        gram = mul(m, mt)
        scale = 1.9 / jnp.max(jnp.sum(jnp.abs(gram), axis=1, keepdims=True), axis=0, keepdims=True)
        state += [mt * scale, eye - gram * scale]

    def size(st):
        worst = jnp.maximum(jnp.abs(st[1]), jnp.abs(st[3]))
        return jnp.max(worst)

    def step(st):
        out = []
        for x, r in ((st[0], st[1]), (st[2], st[3])):
            both = mul(jnp.concatenate([x, r], axis=0), r)
            out += [x + both[:128], both[128:]]
        return out

    def body(carry):
        st = list(carry[2:])
        st = step(st)
        return (carry[0] + 1, size(st), *st)

    st = state
    for _ in range(6):
        st = step(st)
    final = lax.while_loop(
        lambda c: jnp.logical_and(c[0] < LIMIT, c[1] > 1e-4), body, (jnp.int32(0), size(st), *st)
    )
    out = []
    for m, x in zip(mats, (final[2], final[4])):
        out.append(x + mul(x, eye - mul(m, x)))
    return out


def merge_kernel(g, own, out):
    me = lax.axis_index("leaf")
    s, q = me % 2, me // 2 % 2
    left64 = lanes_of((64, 128)) < 64
    left128 = lanes_of((128, 128)) < 64
    pairs = (q, 1 - q)
    zero = jnp.zeros((64, 128), F32)
    mats = []
    for p in pairs:
        sums = [g[p, 0, l, 0, :, 256:384] + g[p, 1, l, 0, :, 256:384] for l in range(2)]
        mats.append(
            jnp.concatenate(
                [jnp.where(left64, sums[0], zero), jnp.where(left64, zero, turn(sums[1]))], axis=0
            )
        )
    inverses = invert(mats)
    weights = []
    for p, inverse, extra in zip(pairs, inverses, (True, False)):
        rows = [
            jnp.where(left64, g[p, e, 0, 1, :, 256:384], turn(g[p, e, 1, 1, :, 256:384])) for e in range(2)
        ]
        if extra:
            rows.append(jnp.where(left128, own[0, :, 256:384], turn(own[1, :, 256:384])))
        weights.append(mul(jnp.concatenate(rows, axis=0), inverse))

    schur, coupled, keep_outer, keep_inner = [], [], [], []
    for l in range(2):
        inner_tiles, outer_parts = [], []
        for p, w, extra in zip(pairs, weights, (True, False)):
            wl = w if l == 0 else turn(w)
            left = lanes_of(wl.shape) < 64
            hi = wl.astype(BF16).astype(F32)
            lo = wl - hi
            lhs = jnp.concatenate(
                [jnp.where(left, hi, turn(lo)).astype(BF16), jnp.where(left, hi, 0.0).astype(BF16)], axis=1
            )
            joint = jnp.where(left64, turn(g[p, 0, l, 0, :, 256:384]), g[p, 1, l, 0, :, 256:384])
            right = jnp.concatenate([g[p, 0, l, 0, :, 0:256], g[p, 1, l, 0, :, 0:256], joint], axis=1)
            bh, bl = split(right)
            prod = dot(lhs, jnp.concatenate([bh, bh, bl, bl], axis=0))
            zeros = jnp.zeros((64, 256), F32)
            base = jnp.concatenate(
                [
                    jnp.concatenate(
                        [
                            g[p, 0, l, 1, :, 0:256],
                            zeros,
                            jnp.where(left64, turn(g[p, 0, l, 1, :, 256:384]), zero),
                        ],
                        axis=1,
                    ),
                    jnp.concatenate(
                        [zeros, g[p, 1, l, 1, :, 0:256], jnp.where(left64, zero, g[p, 1, l, 1, :, 256:384])],
                        axis=1,
                    ),
                ],
                axis=0,
            )
            rows = base - prod[:128]
            outer_parts.append(rows[:, :512])
            inner_tiles.append(rows[:, 512:])
            if extra:
                first = s == 0
                mine = own[l, :, 0:256]
                face = own[l, :, 256:384]
                keep_outer.append(
                    jnp.concatenate([jnp.where(first, mine, 0.0), jnp.where(first, 0.0, mine)], axis=1)
                    - prod[128:, :512]
                )
                placed = jnp.where(
                    left128, jnp.where(first, turn(face), 0.0), jnp.where(first, 0.0, face)
                )
                keep_inner.append(placed - prod[128:, 512:])
        schur.append(inner_tiles[0] + inner_tiles[1])
        coupled.append(outer_parts)
    inverses = invert(schur)
    here = pl.ds(pl.multiple_of(q * 512, 512), 512)
    there = pl.ds(pl.multiple_of((1 - q) * 512, 512), 512)
    for l in range(2):
        w = mul(keep_inner[l], inverses[l])
        out[l, :, here] = keep_outer[l] - mul(w, coupled[l][0])
        out[l, :, there] = -mul(w, coupled[l][1])


def local(solve_ops, inner_deriv, boundary_diag, wall_stencil, wall_coef, cut_faces):
    leaves, inner, bound = solve_ops.shape
    faces, _, half, _ = inner_deriv.shape
    vmem = pl.BlockSpec(memory_space=pltpu.VMEM)
    smem = pl.BlockSpec(memory_space=pltpu.SMEM)
    g, own = pl.pallas_call(
        gather_kernel,
        out_shape=(
            jax.ShapeDtypeStruct((2, 2, leaves, 2, 2 * half, bound), F32),
            jax.ShapeDtypeStruct((leaves, 4 * half, bound), F32),
        ),
        in_specs=[vmem, vmem, vmem, vmem, smem, smem],
        out_specs=(vmem, vmem),
        scratch_shapes=[pltpu.SemaphoreType.DMA((14,)), pltpu.SemaphoreType.DMA((14,))],
        compiler_params=pltpu.CompilerParams(
            collective_id=0, has_side_effects=True, vmem_limit_bytes=32 * 1024 * 1024
        ),
        name="gather_rows",
    )(solve_ops, inner_deriv, boundary_diag, wall_stencil, wall_coef, cut_faces)
    merged = pl.pallas_call(
        merge_kernel,
        out_shape=jax.ShapeDtypeStruct((leaves, 4 * half, 16 * 2 * half), F32),
        in_specs=[vmem, vmem],
        out_specs=vmem,
        compiler_params=pltpu.CompilerParams(vmem_limit_bytes=48 * 1024 * 1024),
        name="merge_levels",
    )(g, own)
    return merged.reshape(leaves, 4, 1, half, 16 * 2 * half)


def solution(mesh):
    in_specs = (
        P("leaf", None, None),
        P(None, "face", None, None),
        P(None, "face", None),
        P("face", None, None),
        P("leaf", None),
        P("leaf", None),
    )
    out_specs = P("leaf", None, "face", None, None)
    return jax.shard_map(local, mesh=mesh, in_specs=in_specs, out_specs=out_specs, check_vma=False)
```

```python
import functools

import jax
import jax.numpy as jnp
from jax import lax
from jax.experimental import pallas as pl
from jax.experimental.pallas import tpu as pltpu
from jax.sharding import PartitionSpec as P

MESH = pl.DeviceIdType.MESH
F32 = jnp.float32
BF16 = jnp.bfloat16
LIMIT = 60


def lanes_of(shape):
    return lax.broadcasted_iota(jnp.int32, shape, len(shape) - 1)


def turn(x):
    return pltpu.roll(x, 64, 1)


def leaf_rows(values, diag, stencil, weights, faces, core, s, q):
    half = 32
    lane = lanes_of((half, 128))
    row = lax.broadcasted_iota(jnp.int32, (half, 128), 0)
    tiles = []
    for n, face in enumerate(faces):
        part = values[n * half : (n + 1) * half]
        side = face % 2
        spot = lane - side * 64
        extra = jnp.where(spot == core * half + row, diag[n], 0.0)
        on = jnp.logical_and(spot >= 0, spot < 64)
        extra = extra + jnp.where(on, stencil * weights[n], 0.0)
        tiles.append(
            [part[:, t * 128 : t * 128 + 128] + jnp.where(face // 2 == t, extra, 0.0) for t in range(3)]
        )
    xt, yt, zt = (jnp.concatenate([row_tiles[t] for row_tiles in tiles], axis=0) for t in range(3))
    left = lanes_of(xt.shape) < 64
    xr, yr = turn(xt), turn(yt)
    first, lower = s == 0, q == 0
    outer = jnp.where(left, jnp.where(first, xt, xr), jnp.where(lower, yr, yt))
    inner = jnp.where(left, jnp.where(first, xr, xt), jnp.where(lower, yt, yr))
    return outer, zt, inner


def gather_kernel(*refs):
    sources, (g, own, send, recv), held, arrive = refs[:6], refs[6:10], refs[10:16], refs[16]
    solve, deriv, diag, stencil, coef, cut = held
    loads = [
        pltpu.make_async_copy(src, dst, arrive.at[n]) for n, (src, dst) in enumerate(zip(sources, held))
    ]
    for load in loads:
        load.start()
    me = lax.axis_index("leaf")
    core = lax.axis_index("face")
    s, q = me % 2, me // 2 % 2
    xdev = (me + 1 - 2 * s, core)
    ydev = (me + 2 - 4 * q, core)
    cdev = (me, 1 - core)
    barrier = pltpu.get_barrier_semaphore()
    for dev in (xdev, ydev, cdev):
        pl.semaphore_signal(barrier, inc=1, device_id=dev, device_id_type=MESH)

    rows = pl.ds(pl.multiple_of(core * 32, 32), 32)

    def copy(index, qq, ss, l, dev):
        where = g.at[qq, ss, l, :, rows, :]
        return pltpu.make_async_remote_copy(
            src_ref=where, dst_ref=where, send_sem=send.at[index], recv_sem=recv.at[index],
            device_id=dev, device_id_type=MESH,
        )

    for load in loads:
        load.wait()
    st = stencil[0]
    st = jnp.concatenate([st, st], axis=1)

    def compute(l, faces):
        d = jnp.concatenate([deriv[f, 0] for f in faces], axis=0)
        values = jnp.dot(d, solve[l], preferred_element_type=F32)
        dd = [jnp.concatenate([diag[f]] * 4, axis=1) for f in faces]
        w = [cut[l, f].astype(F32) * coef[l, f] for f in faces]
        return leaf_rows(values, dd, st, w, faces, core, s, q)

    shared = (1 - s, 3 - q)
    x0, y1 = copy(0, q, s, 0, xdev), copy(1, q, s, 1, ydev)
    x1, y0 = copy(2, q, s, 1, xdev), copy(3, q, s, 0, ydev)
    c0, c1 = copy(4, q, s, 0, cdev), copy(5, q, s, 1, cdev)
    started = [x0, y0, c0, y1, x1, c1]
    for l in range(2):
        for t, tile in enumerate(compute(l, shared)):
            g[q, s, l, 0, rows, t * 128 : t * 128 + 128] = tile[:32]
            g[q, s, l, 1, rows, t * 128 : t * 128 + 128] = tile[32:]
        if l == 0:
            pl.semaphore_wait(barrier, 3)
        for one in started[3 * l : 3 * l + 3]:
            one.start()
    kept = (s, 2 + q, 4, 5)
    for l in range(2):
        for t, tile in enumerate(compute(l, kept)):
            own[l, :, t * 128 : t * 128 + 128] = tile
    later = [
        (x0, [(6, q, 1 - s, 0, ydev), (7, q, 1 - s, 0, cdev)]),
        (y1, [(8, 1 - q, s, 1, xdev), (9, 1 - q, s, 1, cdev)]),
        (x1, [(10, q, 1 - s, 1, cdev)]),
        (y0, [(11, 1 - q, s, 0, cdev)]),
    ]
    done = {}
    for first, relays in later:
        first.wait_recv()
        for relay in relays:
            done[relay[0]] = copy(*relay)
            done[relay[0]].start()
    done[6].wait_recv()
    done[12] = copy(12, 1 - q, 1 - s, 0, cdev)
    done[12].start()
    done[8].wait_recv()
    done[13] = copy(13, 1 - q, 1 - s, 1, cdev)
    done[13].start()
    c0.wait_recv()
    c1.wait_recv()
    for index in (7, 9, 10, 11, 12, 13):
        done[index].wait_recv()
    for one in started + list(done.values()):
        one.wait_send()


def split(x):
    hi = x.astype(BF16)
    return hi, (x - hi.astype(F32)).astype(BF16)


def dot(a, b):
    return jnp.dot(a, b, preferred_element_type=F32)


def mul(a, b):
    ah, al = split(a)
    bh, bl = split(b)
    both = jnp.concatenate([ah, al], axis=1)
    if b.shape[1] == 128:
        weights = jnp.concatenate(
            [jnp.concatenate([bh, bl], axis=1), jnp.concatenate([bh, jnp.zeros_like(bl)], axis=1)], axis=0
        )
        out = dot(both, weights)
        return out[:, :128] + out[:, 128:]
    return dot(both, jnp.concatenate([bh, bh], axis=0)) + dot(ah, bl)


def invert(mats):
    row = lax.broadcasted_iota(jnp.int32, (128, 128), 0)
    eye = (row == lanes_of((128, 128))).astype(F32)
    state = []
    for m in mats:
        mt = m.T
        gram = mul(m, mt)
        scale = 1.9 / jnp.max(jnp.sum(jnp.abs(gram), axis=1, keepdims=True), axis=0, keepdims=True)
        state += [mt * scale, eye - gram * scale]

    def size(st):
        worst = jnp.maximum(jnp.abs(st[1]), jnp.abs(st[3]))
        return jnp.max(worst)

    def step(st):
        out = []
        for x, r in ((st[0], st[1]), (st[2], st[3])):
            both = mul(jnp.concatenate([x, r], axis=0), r)
            out += [x + both[:128], both[128:]]
        return out

    def body(carry):
        st = list(carry[2:])
        st = step(st)
        return (carry[0] + 1, size(st), *st)

    st = state
    for _ in range(6):
        st = step(st)
    final = lax.while_loop(
        lambda c: jnp.logical_and(c[0] < LIMIT, c[1] > 1e-4), body, (jnp.int32(0), size(st), *st)
    )
    out = []
    for m, x in zip(mats, (final[2], final[4])):
        out.append(x + mul(x, eye - mul(m, x)))
    return out


def merge_kernel(g, own, result, out, sems):
    me = lax.axis_index("leaf")
    s, q = me % 2, me // 2 % 2
    left64 = lanes_of((64, 128)) < 64
    left128 = lanes_of((128, 128)) < 64
    pairs = (q, 1 - q)
    zero = jnp.zeros((64, 128), F32)
    mats = []
    for p in pairs:
        sums = [g[p, 0, l, 0, :, 256:384] + g[p, 1, l, 0, :, 256:384] for l in range(2)]
        mats.append(
            jnp.concatenate(
                [jnp.where(left64, sums[0], zero), jnp.where(left64, zero, turn(sums[1]))], axis=0
            )
        )
    inverses = invert(mats)
    weights = []
    for p, inverse, extra in zip(pairs, inverses, (True, False)):
        rows = [
            jnp.where(left64, g[p, e, 0, 1, :, 256:384], turn(g[p, e, 1, 1, :, 256:384])) for e in range(2)
        ]
        if extra:
            rows.append(jnp.where(left128, own[0, :, 256:384], turn(own[1, :, 256:384])))
        weights.append(mul(jnp.concatenate(rows, axis=0), inverse))

    schur, coupled, keep_outer, keep_inner = [], [], [], []
    for l in range(2):
        inner_tiles, outer_parts = [], []
        for p, w, extra in zip(pairs, weights, (True, False)):
            wl = w if l == 0 else turn(w)
            left = lanes_of(wl.shape) < 64
            hi = wl.astype(BF16).astype(F32)
            lo = wl - hi
            lhs = jnp.concatenate(
                [jnp.where(left, hi, turn(lo)).astype(BF16), jnp.where(left, hi, 0.0).astype(BF16)], axis=1
            )
            joint = jnp.where(left64, turn(g[p, 0, l, 0, :, 256:384]), g[p, 1, l, 0, :, 256:384])
            right = jnp.concatenate([g[p, 0, l, 0, :, 0:256], g[p, 1, l, 0, :, 0:256], joint], axis=1)
            bh, bl = split(right)
            prod = dot(lhs, jnp.concatenate([bh, bh, bl, bl], axis=0))
            zeros = jnp.zeros((64, 256), F32)
            base = jnp.concatenate(
                [
                    jnp.concatenate(
                        [
                            g[p, 0, l, 1, :, 0:256],
                            zeros,
                            jnp.where(left64, turn(g[p, 0, l, 1, :, 256:384]), zero),
                        ],
                        axis=1,
                    ),
                    jnp.concatenate(
                        [zeros, g[p, 1, l, 1, :, 0:256], jnp.where(left64, zero, g[p, 1, l, 1, :, 256:384])],
                        axis=1,
                    ),
                ],
                axis=0,
            )
            rows = base - prod[:128]
            outer_parts.append(rows[:, :512])
            inner_tiles.append(rows[:, 512:])
            if extra:
                first = s == 0
                mine = own[l, :, 0:256]
                face = own[l, :, 256:384]
                keep_outer.append(
                    jnp.concatenate([jnp.where(first, mine, 0.0), jnp.where(first, 0.0, mine)], axis=1)
                    - prod[128:, :512]
                )
                placed = jnp.where(
                    left128, jnp.where(first, turn(face), 0.0), jnp.where(first, 0.0, face)
                )
                keep_inner.append(placed - prod[128:, 512:])
        schur.append(inner_tiles[0] + inner_tiles[1])
        coupled.append(outer_parts)
    inverses = invert(schur)
    here = pl.ds(pl.multiple_of(q * 512, 512), 512)
    there = pl.ds(pl.multiple_of((1 - q) * 512, 512), 512)
    copies = []
    for l in range(2):
        w = mul(keep_inner[l], inverses[l])
        for part, place in enumerate((here, there)):
            value = mul(w, coupled[l][part])
            out[2 * l + part] = keep_outer[l] - value if part == 0 else -value
            one = pltpu.make_async_copy(out.at[2 * l + part], result.at[l, :, place], sems.at[2 * l + part])
            one.start()
            copies.append(one)
    for one in copies:
        one.wait()


def local(solve_ops, inner_deriv, boundary_diag, wall_stencil, wall_coef, cut_faces):
    leaves, inner, bound = solve_ops.shape
    faces, _, half, _ = inner_deriv.shape
    vmem = pl.BlockSpec(memory_space=pltpu.VMEM)
    hbm = pl.BlockSpec(memory_space=pltpu.HBM)
    arrays = (solve_ops, inner_deriv, boundary_diag, wall_stencil, wall_coef, cut_faces)
    g, own = pl.pallas_call(
        gather_kernel,
        out_shape=(
            jax.ShapeDtypeStruct((2, 2, leaves, 2, 2 * half, bound), F32),
            jax.ShapeDtypeStruct((leaves, 4 * half, bound), F32),
        ),
        in_specs=[hbm] * 6,
        out_specs=(vmem, vmem),
        scratch_shapes=[pltpu.SemaphoreType.DMA((14,)), pltpu.SemaphoreType.DMA((14,))]
        + [pltpu.VMEM(a.shape, a.dtype) for a in arrays[:4]]
        + [pltpu.SMEM(a.shape, a.dtype) for a in arrays[4:]]
        + [pltpu.SemaphoreType.DMA((6,))],
        compiler_params=pltpu.CompilerParams(
            collective_id=0, has_side_effects=True, vmem_limit_bytes=45056 * 1024
        ),
        name="gather_rows",
    )(*arrays)
    merged = pl.pallas_call(
        merge_kernel,
        out_shape=jax.ShapeDtypeStruct((leaves, 4 * half, 16 * 2 * half), F32),
        in_specs=[vmem, vmem],
        out_specs=hbm,
        scratch_shapes=[pltpu.VMEM((2 * leaves, 4 * half, 8 * 2 * half), F32), pltpu.SemaphoreType.DMA((4,))],
        compiler_params=pltpu.CompilerParams(vmem_limit_bytes=48 * 1024 * 1024),
        name="merge_levels",
    )(g, own)
    return merged.reshape(leaves, 4, 1, half, 16 * 2 * half)


def solution(mesh):
    in_specs = (
        P("leaf", None, None),
        P(None, "face", None, None),
        P(None, "face", None),
        P("face", None, None),
        P("leaf", None),
        P("leaf", None),
    )
    out_specs = P("leaf", None, "face", None, None)
    return jax.shard_map(local, mesh=mesh, in_specs=in_specs, out_specs=out_specs, check_vma=False)
```

```python
import functools

import jax
import jax.numpy as jnp
from jax import lax
from jax.experimental import pallas as pl
from jax.experimental.pallas import tpu as pltpu
from jax.sharding import PartitionSpec as P

MESH = pl.DeviceIdType.MESH
F32 = jnp.float32
BF16 = jnp.bfloat16
LIMIT = 60


def lanes_of(shape):
    return lax.broadcasted_iota(jnp.int32, shape, len(shape) - 1)


def turn(x):
    return pltpu.roll(x, 64, 1)


def leaf_rows(values, diag, stencil, weights, faces, core, s, q):
    half = 32
    lane = lanes_of((half, 128))
    row = lax.broadcasted_iota(jnp.int32, (half, 128), 0)
    tiles = []
    for n, face in enumerate(faces):
        part = values[n * half : (n + 1) * half]
        side = face % 2
        spot = lane - side * 64
        extra = jnp.where(spot == core * half + row, diag[n], 0.0)
        on = jnp.logical_and(spot >= 0, spot < 64)
        extra = extra + jnp.where(on, stencil * weights[n], 0.0)
        tiles.append(
            [part[:, t * 128 : t * 128 + 128] + jnp.where(face // 2 == t, extra, 0.0) for t in range(3)]
        )
    xt, yt, zt = (jnp.concatenate([row_tiles[t] for row_tiles in tiles], axis=0) for t in range(3))
    left = lanes_of(xt.shape) < 64
    xr, yr = turn(xt), turn(yt)
    first, lower = s == 0, q == 0
    outer = jnp.where(left, jnp.where(first, xt, xr), jnp.where(lower, yr, yt))
    inner = jnp.where(left, jnp.where(first, xr, xt), jnp.where(lower, yt, yr))
    return outer, zt, inner


def gather_kernel(*refs):
    sources, (g_out, own_out, send, recv), held, (arrive, g, own, leave) = (
        refs[:6], refs[6:10], refs[10:16], refs[16:]
    )
    solve, deriv, diag, stencil, coef, cut = held
    loads = [
        pltpu.make_async_copy(src, dst, arrive.at[n]) for n, (src, dst) in enumerate(zip(sources, held))
    ]
    for load in loads:
        load.start()
    me = lax.axis_index("leaf")
    core = lax.axis_index("face")
    s, q = me % 2, me // 2 % 2
    xdev = (me + 1 - 2 * s, core)
    ydev = (me + 2 - 4 * q, core)
    cdev = (me, 1 - core)
    barrier = pltpu.get_barrier_semaphore()
    for dev in (xdev, ydev, cdev):
        pl.semaphore_signal(barrier, inc=1, device_id=dev, device_id_type=MESH)

    rows = pl.ds(pl.multiple_of(core * 32, 32), 32)

    def copy(index, qq, ss, l, dev):
        where = g.at[qq, ss, l, :, rows, :]
        return pltpu.make_async_remote_copy(
            src_ref=where, dst_ref=where, send_sem=send.at[index], recv_sem=recv.at[index],
            device_id=dev, device_id_type=MESH,
        )

    for load in loads:
        load.wait()
    st = stencil[0]
    st = jnp.concatenate([st, st], axis=1)

    def compute(l, faces):
        d = jnp.concatenate([deriv[f, 0] for f in faces], axis=0)
        values = jnp.dot(d, solve[l], preferred_element_type=F32)
        dd = [jnp.concatenate([diag[f]] * 4, axis=1) for f in faces]
        w = [cut[l, f].astype(F32) * coef[l, f] for f in faces]
        return leaf_rows(values, dd, st, w, faces, core, s, q)

    shared = (1 - s, 3 - q)
    x0, y1 = copy(0, q, s, 0, xdev), copy(1, q, s, 1, ydev)
    x1, y0 = copy(2, q, s, 1, xdev), copy(3, q, s, 0, ydev)
    c0, c1 = copy(4, q, s, 0, cdev), copy(5, q, s, 1, cdev)
    started = [x0, y0, c0, y1, x1, c1]
    for l in range(2):
        for t, tile in enumerate(compute(l, shared)):
            g[q, s, l, 0, rows, t * 128 : t * 128 + 128] = tile[:32]
            g[q, s, l, 1, rows, t * 128 : t * 128 + 128] = tile[32:]
        if l == 0:
            pl.semaphore_wait(barrier, 3)
        for one in started[3 * l : 3 * l + 3]:
            one.start()
    kept = (s, 2 + q, 4, 5)
    for l in range(2):
        for t, tile in enumerate(compute(l, kept)):
            own[l, :, t * 128 : t * 128 + 128] = tile
    stored = [pltpu.make_async_copy(own, own_out, leave.at[8])]
    stored[0].start()

    def store(index, qq, ss, l):
        one = pltpu.make_async_copy(g.at[qq, ss, l], g_out.at[qq, ss, l], leave.at[index])
        one.start()
        stored.append(one)

    later = [
        (x0, [(6, q, 1 - s, 0, ydev), (7, q, 1 - s, 0, cdev)]),
        (y1, [(8, 1 - q, s, 1, xdev), (9, 1 - q, s, 1, cdev)]),
        (x1, [(10, q, 1 - s, 1, cdev)]),
        (y0, [(11, 1 - q, s, 0, cdev)]),
    ]
    done = {}
    for first, relays in later:
        first.wait_recv()
        for relay in relays:
            done[relay[0]] = copy(*relay)
            done[relay[0]].start()
    c0.wait_recv()
    store(0, q, s, 0)
    c1.wait_recv()
    store(1, q, s, 1)
    done[7].wait_recv()
    store(2, q, 1 - s, 0)
    done[9].wait_recv()
    store(3, 1 - q, s, 1)
    done[10].wait_recv()
    store(4, q, 1 - s, 1)
    done[11].wait_recv()
    store(5, 1 - q, s, 0)
    done[6].wait_recv()
    done[12] = copy(12, 1 - q, 1 - s, 0, cdev)
    done[12].start()
    done[8].wait_recv()
    done[13] = copy(13, 1 - q, 1 - s, 1, cdev)
    done[13].start()
    done[12].wait_recv()
    store(6, 1 - q, 1 - s, 0)
    done[13].wait_recv()
    store(7, 1 - q, 1 - s, 1)
    for one in started + list(done.values()):
        one.wait_send()
    for one in stored:
        one.wait()


def split(x):
    hi = x.astype(BF16)
    return hi, (x - hi.astype(F32)).astype(BF16)


def dot(a, b):
    return jnp.dot(a, b, preferred_element_type=F32)


def mul(a, b):
    ah, al = split(a)
    bh, bl = split(b)
    both = jnp.concatenate([ah, al], axis=1)
    if b.shape[1] == 128:
        weights = jnp.concatenate(
            [jnp.concatenate([bh, bl], axis=1), jnp.concatenate([bh, jnp.zeros_like(bl)], axis=1)], axis=0
        )
        out = dot(both, weights)
        return out[:, :128] + out[:, 128:]
    return dot(both, jnp.concatenate([bh, bh], axis=0)) + dot(ah, bl)


def invert(mats):
    row = lax.broadcasted_iota(jnp.int32, (128, 128), 0)
    eye = (row == lanes_of((128, 128))).astype(F32)
    state = []
    for m in mats:
        mt = m.T
        gram = mul(m, mt)
        scale = 1.9 / jnp.max(jnp.sum(jnp.abs(gram), axis=1, keepdims=True), axis=0, keepdims=True)
        state += [mt * scale, eye - gram * scale]

    def size(st):
        worst = jnp.maximum(jnp.abs(st[1]), jnp.abs(st[3]))
        return jnp.max(worst)

    def step(st):
        out = []
        for x, r in ((st[0], st[1]), (st[2], st[3])):
            both = mul(jnp.concatenate([x, r], axis=0), r)
            out += [x + both[:128], both[128:]]
        return out

    def body(carry):
        st = list(carry[2:])
        st = step(st)
        return (carry[0] + 1, size(st), *st)

    st = state
    for _ in range(6):
        st = step(st)
    final = lax.while_loop(
        lambda c: jnp.logical_and(c[0] < LIMIT, c[1] > 1e-4), body, (jnp.int32(0), size(st), *st)
    )
    out = []
    for m, x in zip(mats, (final[2], final[4])):
        out.append(x + mul(x, eye - mul(m, x)))
    return out


def merge_kernel(g_in, own_in, result, out, sems, g, own, arrive):
    early = [
        pltpu.make_async_copy(
            g_in.at[:, :, :, 0, :, 256:384], g.at[:, :, :, 0, :, 256:384], arrive.at[0]
        )
    ]
    late = [
        pltpu.make_async_copy(g_in.at[:, :, :, 1], g.at[:, :, :, 1], arrive.at[1]),
        pltpu.make_async_copy(
            g_in.at[:, :, :, 0, :, 0:256], g.at[:, :, :, 0, :, 0:256], arrive.at[2]
        ),
        pltpu.make_async_copy(own_in, own, arrive.at[3]),
    ]
    for load in early + late:
        load.start()
    early[0].wait()
    me = lax.axis_index("leaf")
    s, q = me % 2, me // 2 % 2
    left64 = lanes_of((64, 128)) < 64
    left128 = lanes_of((128, 128)) < 64
    pairs = (q, 1 - q)
    zero = jnp.zeros((64, 128), F32)
    mats = []
    for p in pairs:
        sums = [g[p, 0, l, 0, :, 256:384] + g[p, 1, l, 0, :, 256:384] for l in range(2)]
        mats.append(
            jnp.concatenate(
                [jnp.where(left64, sums[0], zero), jnp.where(left64, zero, turn(sums[1]))], axis=0
            )
        )
    inverses = invert(mats)
    for load in late:
        load.wait()
    weights = []
    for p, inverse, extra in zip(pairs, inverses, (True, False)):
        rows = [
            jnp.where(left64, g[p, e, 0, 1, :, 256:384], turn(g[p, e, 1, 1, :, 256:384])) for e in range(2)
        ]
        if extra:
            rows.append(jnp.where(left128, own[0, :, 256:384], turn(own[1, :, 256:384])))
        weights.append(mul(jnp.concatenate(rows, axis=0), inverse))

    schur, coupled, keep_outer, keep_inner = [], [], [], []
    for l in range(2):
        inner_tiles, outer_parts = [], []
        for p, w, extra in zip(pairs, weights, (True, False)):
            wl = w if l == 0 else turn(w)
            left = lanes_of(wl.shape) < 64
            hi = wl.astype(BF16).astype(F32)
            lo = wl - hi
            lhs = jnp.concatenate(
                [jnp.where(left, hi, turn(lo)).astype(BF16), jnp.where(left, hi, 0.0).astype(BF16)], axis=1
            )
            joint = jnp.where(left64, turn(g[p, 0, l, 0, :, 256:384]), g[p, 1, l, 0, :, 256:384])
            right = jnp.concatenate([g[p, 0, l, 0, :, 0:256], g[p, 1, l, 0, :, 0:256], joint], axis=1)
            bh, bl = split(right)
            prod = dot(lhs, jnp.concatenate([bh, bh, bl, bl], axis=0))
            zeros = jnp.zeros((64, 256), F32)
            base = jnp.concatenate(
                [
                    jnp.concatenate(
                        [
                            g[p, 0, l, 1, :, 0:256],
                            zeros,
                            jnp.where(left64, turn(g[p, 0, l, 1, :, 256:384]), zero),
                        ],
                        axis=1,
                    ),
                    jnp.concatenate(
                        [zeros, g[p, 1, l, 1, :, 0:256], jnp.where(left64, zero, g[p, 1, l, 1, :, 256:384])],
                        axis=1,
                    ),
                ],
                axis=0,
            )
            rows = base - prod[:128]
            outer_parts.append(rows[:, :512])
            inner_tiles.append(rows[:, 512:])
            if extra:
                first = s == 0
                mine = own[l, :, 0:256]
                face = own[l, :, 256:384]
                keep_outer.append(
                    jnp.concatenate([jnp.where(first, mine, 0.0), jnp.where(first, 0.0, mine)], axis=1)
                    - prod[128:, :512]
                )
                placed = jnp.where(
                    left128, jnp.where(first, turn(face), 0.0), jnp.where(first, 0.0, face)
                )
                keep_inner.append(placed - prod[128:, 512:])
        schur.append(inner_tiles[0] + inner_tiles[1])
        coupled.append(outer_parts)
    inverses = invert(schur)
    here = pl.ds(pl.multiple_of(q * 512, 512), 512)
    there = pl.ds(pl.multiple_of((1 - q) * 512, 512), 512)
    copies = []
    for l in range(2):
        w = mul(keep_inner[l], inverses[l])
        for part, place in enumerate((here, there)):
            value = mul(w, coupled[l][part])
            out[2 * l + part] = keep_outer[l] - value if part == 0 else -value
            one = pltpu.make_async_copy(out.at[2 * l + part], result.at[l, :, place], sems.at[2 * l + part])
            one.start()
            copies.append(one)
    for one in copies:
        one.wait()


def local(solve_ops, inner_deriv, boundary_diag, wall_stencil, wall_coef, cut_faces):
    leaves, inner, bound = solve_ops.shape
    faces, _, half, _ = inner_deriv.shape
    hbm = pl.BlockSpec(memory_space=pltpu.HBM)
    arrays = (solve_ops, inner_deriv, boundary_diag, wall_stencil, wall_coef, cut_faces)
    g, own = pl.pallas_call(
        gather_kernel,
        out_shape=(
            jax.ShapeDtypeStruct((2, 2, leaves, 2, 2 * half, bound), F32),
            jax.ShapeDtypeStruct((leaves, 4 * half, bound), F32),
        ),
        in_specs=[hbm] * 6,
        out_specs=(hbm, hbm),
        scratch_shapes=[pltpu.SemaphoreType.DMA((14,)), pltpu.SemaphoreType.DMA((14,))]
        + [pltpu.VMEM(a.shape, a.dtype) for a in arrays[:4]]
        + [pltpu.SMEM(a.shape, a.dtype) for a in arrays[4:]]
        + [
            pltpu.SemaphoreType.DMA((6,)),
            pltpu.VMEM((2, 2, leaves, 2, 2 * half, bound), F32),
            pltpu.VMEM((leaves, 4 * half, bound), F32),
            pltpu.SemaphoreType.DMA((9,)),
        ],
        compiler_params=pltpu.CompilerParams(
            collective_id=0, has_side_effects=True, vmem_limit_bytes=60 * 1024 * 1024
        ),
        name="gather_rows",
    )(*arrays)
    merged = pl.pallas_call(
        merge_kernel,
        out_shape=jax.ShapeDtypeStruct((leaves, 4 * half, 16 * 2 * half), F32),
        in_specs=[hbm, hbm],
        out_specs=hbm,
        scratch_shapes=[
            pltpu.VMEM((2 * leaves, 4 * half, 8 * 2 * half), F32),
            pltpu.SemaphoreType.DMA((4,)),
            pltpu.VMEM(g.shape, F32),
            pltpu.VMEM(own.shape, F32),
            pltpu.SemaphoreType.DMA((4,)),
        ],
        compiler_params=pltpu.CompilerParams(vmem_limit_bytes=60 * 1024 * 1024),
        name="merge_levels",
    )(g, own)
    return merged.reshape(leaves, 4, 1, half, 16 * 2 * half)


def solution(mesh):
    in_specs = (
        P("leaf", None, None),
        P(None, "face", None, None),
        P(None, "face", None),
        P("face", None, None),
        P("leaf", None),
        P("leaf", None),
    )
    out_specs = P("leaf", None, "face", None, None)
    return jax.shard_map(local, mesh=mesh, in_specs=in_specs, out_specs=out_specs, check_vma=False)
```

```python
import functools

import jax
import jax.numpy as jnp
from jax import lax
from jax.experimental import pallas as pl
from jax.experimental.pallas import tpu as pltpu
from jax.sharding import PartitionSpec as P

MESH = pl.DeviceIdType.MESH
F32 = jnp.float32
BF16 = jnp.bfloat16
LIMIT = 60


def lanes_of(shape):
    return lax.broadcasted_iota(jnp.int32, shape, len(shape) - 1)


def turn(x):
    return pltpu.roll(x, 64, 1)


def leaf_rows(values, diag, stencil, weights, faces, core, s, q):
    half = 32
    lane = lanes_of((half, 128))
    row = lax.broadcasted_iota(jnp.int32, (half, 128), 0)
    tiles = []
    for n, face in enumerate(faces):
        part = values[n * half : (n + 1) * half]
        side = face % 2
        spot = lane - side * 64
        extra = jnp.where(spot == core * half + row, diag[n], 0.0)
        on = jnp.logical_and(spot >= 0, spot < 64)
        extra = extra + jnp.where(on, stencil * weights[n], 0.0)
        tiles.append(
            [part[:, t * 128 : t * 128 + 128] + jnp.where(face // 2 == t, extra, 0.0) for t in range(3)]
        )
    xt, yt, zt = (jnp.concatenate([row_tiles[t] for row_tiles in tiles], axis=0) for t in range(3))
    left = lanes_of(xt.shape) < 64
    xr, yr = turn(xt), turn(yt)
    first, lower = s == 0, q == 0
    outer = jnp.where(left, jnp.where(first, xt, xr), jnp.where(lower, yr, yt))
    inner = jnp.where(left, jnp.where(first, xr, xt), jnp.where(lower, yt, yr))
    return outer, zt, inner


def gather_kernel(*refs):
    sources, (g_out, own_out, send, recv), held, (arrive, g, own, leave) = (
        refs[:6], refs[6:10], refs[10:16], refs[16:]
    )
    solve, deriv, diag, stencil, coef, cut = held
    loads = [
        pltpu.make_async_copy(src, dst, arrive.at[n]) for n, (src, dst) in enumerate(zip(sources, held))
    ]
    for load in loads:
        load.start()
    me = lax.axis_index("leaf")
    core = lax.axis_index("face")
    s, q = me % 2, me // 2 % 2
    xdev = (me + 1 - 2 * s, core)
    ydev = (me + 2 - 4 * q, core)
    cdev = (me, 1 - core)
    barrier = pltpu.get_barrier_semaphore()
    for dev in (xdev, ydev, cdev):
        pl.semaphore_signal(barrier, inc=1, device_id=dev, device_id_type=MESH)

    rows = pl.ds(pl.multiple_of(core * 32, 32), 32)

    def copy(index, qq, ss, l, dev):
        where = g.at[qq, ss, l, :, rows, :]
        return pltpu.make_async_remote_copy(
            src_ref=where, dst_ref=where, send_sem=send.at[index], recv_sem=recv.at[index],
            device_id=dev, device_id_type=MESH,
        )

    for load in loads:
        load.wait()
    st = stencil[0]
    st = jnp.concatenate([st, st], axis=1)

    def compute(l, faces):
        d = jnp.concatenate([deriv[f, 0] for f in faces], axis=0)
        values = jnp.dot(d, solve[l], preferred_element_type=F32)
        dd = [jnp.concatenate([diag[f]] * 4, axis=1) for f in faces]
        w = [cut[l, f].astype(F32) * coef[l, f] for f in faces]
        return leaf_rows(values, dd, st, w, faces, core, s, q)

    shared = (1 - s, 3 - q)
    x0, y1 = copy(0, q, s, 0, xdev), copy(1, q, s, 1, ydev)
    x1, y0 = copy(2, q, s, 1, xdev), copy(3, q, s, 0, ydev)
    c0, c1 = copy(4, q, s, 0, cdev), copy(5, q, s, 1, cdev)
    started = [x0, y1, c0, c1, x1, y0]
    for l in range(2):
        for t, tile in enumerate(compute(l, shared)):
            g[q, s, l, 0, rows, t * 128 : t * 128 + 128] = tile[:32]
            g[q, s, l, 1, rows, t * 128 : t * 128 + 128] = tile[32:]
        if l == 0:
            pl.semaphore_wait(barrier, 3)
            x0.start()
        else:
            y1.start()
            c0.start()
            c1.start()
    kept = (s, 2 + q, 4, 5)
    for l in range(2):
        for t, tile in enumerate(compute(l, kept)):
            own[l, :, t * 128 : t * 128 + 128] = tile
    stored = [pltpu.make_async_copy(own, own_out, leave.at[8])]
    stored[0].start()

    def store(index, qq, ss, l):
        one = pltpu.make_async_copy(g.at[qq, ss, l], g_out.at[qq, ss, l], leave.at[index])
        one.start()
        stored.append(one)

    x0.wait_send()
    x1.start()
    y1.wait_send()
    y0.start()
    later = [
        (x0, [(6, q, 1 - s, 0, ydev), (7, q, 1 - s, 0, cdev)]),
        (y1, [(8, 1 - q, s, 1, xdev), (9, 1 - q, s, 1, cdev)]),
        (x1, [(10, q, 1 - s, 1, cdev)]),
        (y0, [(11, 1 - q, s, 0, cdev)]),
    ]
    done = {}
    for first, relays in later:
        first.wait_recv()
        for relay in relays:
            done[relay[0]] = copy(*relay)
            done[relay[0]].start()
    c0.wait_recv()
    store(0, q, s, 0)
    c1.wait_recv()
    store(1, q, s, 1)
    done[7].wait_recv()
    store(2, q, 1 - s, 0)
    done[9].wait_recv()
    store(3, 1 - q, s, 1)
    done[10].wait_recv()
    store(4, q, 1 - s, 1)
    done[11].wait_recv()
    store(5, 1 - q, s, 0)
    done[6].wait_recv()
    done[12] = copy(12, 1 - q, 1 - s, 0, cdev)
    done[12].start()
    done[8].wait_recv()
    done[13] = copy(13, 1 - q, 1 - s, 1, cdev)
    done[13].start()
    done[12].wait_recv()
    store(6, 1 - q, 1 - s, 0)
    done[13].wait_recv()
    store(7, 1 - q, 1 - s, 1)
    for one in started[2:] + list(done.values()):
        one.wait_send()
    for one in stored:
        one.wait()


def split(x):
    hi = x.astype(BF16)
    return hi, (x - hi.astype(F32)).astype(BF16)


def dot(a, b):
    return jnp.dot(a, b, preferred_element_type=F32)


def mul(a, b):
    ah, al = split(a)
    bh, bl = split(b)
    both = jnp.concatenate([ah, al], axis=1)
    if b.shape[1] == 128:
        weights = jnp.concatenate(
            [jnp.concatenate([bh, bl], axis=1), jnp.concatenate([bh, jnp.zeros_like(bl)], axis=1)], axis=0
        )
        out = dot(both, weights)
        return out[:, :128] + out[:, 128:]
    return dot(both, jnp.concatenate([bh, bh], axis=0)) + dot(ah, bl)


def invert(mats):
    row = lax.broadcasted_iota(jnp.int32, (128, 128), 0)
    eye = (row == lanes_of((128, 128))).astype(F32)
    state = []
    for m in mats:
        mt = m.T
        gram = mul(m, mt)
        scale = 1.9 / jnp.max(jnp.sum(jnp.abs(gram), axis=1, keepdims=True), axis=0, keepdims=True)
        state += [mt * scale, eye - gram * scale]

    def size(st):
        worst = jnp.maximum(jnp.abs(st[1]), jnp.abs(st[3]))
        return jnp.max(worst)

    def step(st):
        out = []
        for x, r in ((st[0], st[1]), (st[2], st[3])):
            both = mul(jnp.concatenate([x, r], axis=0), r)
            out += [x + both[:128], both[128:]]
        return out

    def body(carry):
        st = list(carry[2:])
        st = step(st)
        return (carry[0] + 1, size(st), *st)

    st = state
    for _ in range(6):
        st = step(st)
    final = lax.while_loop(
        lambda c: jnp.logical_and(c[0] < LIMIT, c[1] > 1e-4), body, (jnp.int32(0), size(st), *st)
    )
    out = []
    for m, x in zip(mats, (final[2], final[4])):
        out.append(x + mul(x, eye - mul(m, x)))
    return out


def merge_kernel(g_in, own_in, result, out, sems, g, own, arrive):
    early = [
        pltpu.make_async_copy(
            g_in.at[:, :, :, 0, :, 256:384], g.at[:, :, :, 0, :, 256:384], arrive.at[0]
        )
    ]
    late = [
        pltpu.make_async_copy(g_in.at[:, :, :, 1], g.at[:, :, :, 1], arrive.at[1]),
        pltpu.make_async_copy(
            g_in.at[:, :, :, 0, :, 0:256], g.at[:, :, :, 0, :, 0:256], arrive.at[2]
        ),
        pltpu.make_async_copy(own_in, own, arrive.at[3]),
    ]
    for load in early + late:
        load.start()
    early[0].wait()
    me = lax.axis_index("leaf")
    s, q = me % 2, me // 2 % 2
    left64 = lanes_of((64, 128)) < 64
    left128 = lanes_of((128, 128)) < 64
    pairs = (q, 1 - q)
    zero = jnp.zeros((64, 128), F32)
    mats = []
    for p in pairs:
        sums = [g[p, 0, l, 0, :, 256:384] + g[p, 1, l, 0, :, 256:384] for l in range(2)]
        mats.append(
            jnp.concatenate(
                [jnp.where(left64, sums[0], zero), jnp.where(left64, zero, turn(sums[1]))], axis=0
            )
        )
    inverses = invert(mats)
    for load in late:
        load.wait()
    weights = []
    for p, inverse, extra in zip(pairs, inverses, (True, False)):
        rows = [
            jnp.where(left64, g[p, e, 0, 1, :, 256:384], turn(g[p, e, 1, 1, :, 256:384])) for e in range(2)
        ]
        if extra:
            rows.append(jnp.where(left128, own[0, :, 256:384], turn(own[1, :, 256:384])))
        weights.append(mul(jnp.concatenate(rows, axis=0), inverse))

    schur, coupled, keep_outer, keep_inner = [], [], [], []
    for l in range(2):
        inner_tiles, outer_parts = [], []
        for p, w, extra in zip(pairs, weights, (True, False)):
            wl = w if l == 0 else turn(w)
            left = lanes_of(wl.shape) < 64
            hi = wl.astype(BF16).astype(F32)
            lo = wl - hi
            lhs = jnp.concatenate(
                [jnp.where(left, hi, turn(lo)).astype(BF16), jnp.where(left, hi, 0.0).astype(BF16)], axis=1
            )
            joint = jnp.where(left64, turn(g[p, 0, l, 0, :, 256:384]), g[p, 1, l, 0, :, 256:384])
            right = jnp.concatenate([g[p, 0, l, 0, :, 0:256], g[p, 1, l, 0, :, 0:256], joint], axis=1)
            bh, bl = split(right)
            prod = dot(lhs, jnp.concatenate([bh, bh, bl, bl], axis=0))
            zeros = jnp.zeros((64, 256), F32)
            base = jnp.concatenate(
                [
                    jnp.concatenate(
                        [
                            g[p, 0, l, 1, :, 0:256],
                            zeros,
                            jnp.where(left64, turn(g[p, 0, l, 1, :, 256:384]), zero),
                        ],
                        axis=1,
                    ),
                    jnp.concatenate(
                        [zeros, g[p, 1, l, 1, :, 0:256], jnp.where(left64, zero, g[p, 1, l, 1, :, 256:384])],
                        axis=1,
                    ),
                ],
                axis=0,
            )
            rows = base - prod[:128]
            outer_parts.append(rows[:, :512])
            inner_tiles.append(rows[:, 512:])
            if extra:
                first = s == 0
                mine = own[l, :, 0:256]
                face = own[l, :, 256:384]
                keep_outer.append(
                    jnp.concatenate([jnp.where(first, mine, 0.0), jnp.where(first, 0.0, mine)], axis=1)
                    - prod[128:, :512]
                )
                placed = jnp.where(
                    left128, jnp.where(first, turn(face), 0.0), jnp.where(first, 0.0, face)
                )
                keep_inner.append(placed - prod[128:, 512:])
        schur.append(inner_tiles[0] + inner_tiles[1])
        coupled.append(outer_parts)
    inverses = invert(schur)
    here = pl.ds(pl.multiple_of(q * 512, 512), 512)
    there = pl.ds(pl.multiple_of((1 - q) * 512, 512), 512)
    copies = []
    for l in range(2):
        w = mul(keep_inner[l], inverses[l])
        for part, place in enumerate((here, there)):
            value = mul(w, coupled[l][part])
            out[2 * l + part] = keep_outer[l] - value if part == 0 else -value
            one = pltpu.make_async_copy(out.at[2 * l + part], result.at[l, :, place], sems.at[2 * l + part])
            one.start()
            copies.append(one)
    for one in copies:
        one.wait()


def local(solve_ops, inner_deriv, boundary_diag, wall_stencil, wall_coef, cut_faces):
    leaves, inner, bound = solve_ops.shape
    faces, _, half, _ = inner_deriv.shape
    hbm = pl.BlockSpec(memory_space=pltpu.HBM)
    arrays = (solve_ops, inner_deriv, boundary_diag, wall_stencil, wall_coef, cut_faces)
    g, own = pl.pallas_call(
        gather_kernel,
        out_shape=(
            jax.ShapeDtypeStruct((2, 2, leaves, 2, 2 * half, bound), F32),
            jax.ShapeDtypeStruct((leaves, 4 * half, bound), F32),
        ),
        in_specs=[hbm] * 6,
        out_specs=(hbm, hbm),
        scratch_shapes=[pltpu.SemaphoreType.DMA((14,)), pltpu.SemaphoreType.DMA((14,))]
        + [pltpu.VMEM(a.shape, a.dtype) for a in arrays[:4]]
        + [pltpu.SMEM(a.shape, a.dtype) for a in arrays[4:]]
        + [
            pltpu.SemaphoreType.DMA((6,)),
            pltpu.VMEM((2, 2, leaves, 2, 2 * half, bound), F32),
            pltpu.VMEM((leaves, 4 * half, bound), F32),
            pltpu.SemaphoreType.DMA((9,)),
        ],
        compiler_params=pltpu.CompilerParams(
            collective_id=0, has_side_effects=True, vmem_limit_bytes=60 * 1024 * 1024
        ),
        name="gather_rows",
    )(*arrays)
    merged = pl.pallas_call(
        merge_kernel,
        out_shape=jax.ShapeDtypeStruct((leaves, 4 * half, 16 * 2 * half), F32),
        in_specs=[hbm, hbm],
        out_specs=hbm,
        scratch_shapes=[
            pltpu.VMEM((2 * leaves, 4 * half, 8 * 2 * half), F32),
            pltpu.SemaphoreType.DMA((4,)),
            pltpu.VMEM(g.shape, F32),
            pltpu.VMEM(own.shape, F32),
            pltpu.SemaphoreType.DMA((4,)),
        ],
        compiler_params=pltpu.CompilerParams(vmem_limit_bytes=60 * 1024 * 1024),
        name="merge_levels",
    )(g, own)
    return merged.reshape(leaves, 4, 1, half, 16 * 2 * half)


def solution(mesh):
    in_specs = (
        P("leaf", None, None),
        P(None, "face", None, None),
        P(None, "face", None),
        P("face", None, None),
        P("leaf", None),
        P("leaf", None),
    )
    out_specs = P("leaf", None, "face", None, None)
    return jax.shard_map(local, mesh=mesh, in_specs=in_specs, out_specs=out_specs, check_vma=False)
```

```python
import functools

import jax
import jax.numpy as jnp
from jax import lax
from jax.experimental import pallas as pl
from jax.experimental.pallas import tpu as pltpu
from jax.sharding import PartitionSpec as P

MESH = pl.DeviceIdType.MESH
F32 = jnp.float32
BF16 = jnp.bfloat16
LIMIT = 60


def lanes_of(shape):
    return lax.broadcasted_iota(jnp.int32, shape, len(shape) - 1)


def turn(x):
    return pltpu.roll(x, 64, 1)


def leaf_rows(values, diag, stencil, weights, faces, core, s, q):
    half = 32
    lane = lanes_of((half, 128))
    row = lax.broadcasted_iota(jnp.int32, (half, 128), 0)
    tiles = []
    for n, face in enumerate(faces):
        part = values[n * half : (n + 1) * half]
        side = face % 2
        spot = lane - side * 64
        extra = jnp.where(spot == core * half + row, diag[n], 0.0)
        on = jnp.logical_and(spot >= 0, spot < 64)
        extra = extra + jnp.where(on, stencil * weights[n], 0.0)
        tiles.append(
            [part[:, t * 128 : t * 128 + 128] + jnp.where(face // 2 == t, extra, 0.0) for t in range(3)]
        )
    xt, yt, zt = (jnp.concatenate([row_tiles[t] for row_tiles in tiles], axis=0) for t in range(3))
    left = lanes_of(xt.shape) < 64
    xr, yr = turn(xt), turn(yt)
    first, lower = s == 0, q == 0
    outer = jnp.where(left, jnp.where(first, xt, xr), jnp.where(lower, yr, yt))
    inner = jnp.where(left, jnp.where(first, xr, xt), jnp.where(lower, yt, yr))
    return outer, zt, inner


def gather_kernel(*refs):
    sources, (g_out, own_out, send, recv), held, (arrive, g, own, leave) = (
        refs[:6], refs[6:10], refs[10:16], refs[16:]
    )
    solve, deriv, diag, stencil, coef, cut = held
    loads = [
        pltpu.make_async_copy(src, dst, arrive.at[n]) for n, (src, dst) in enumerate(zip(sources, held))
    ]
    for load in loads:
        load.start()
    me = lax.axis_index("leaf")
    core = lax.axis_index("face")
    s, q = me % 2, me // 2 % 2
    xdev = (me + 1 - 2 * s, core)
    ydev = (me + 2 - 4 * q, core)
    cdev = (me, 1 - core)
    barrier = pltpu.get_barrier_semaphore()
    for dev in (xdev, ydev, cdev):
        pl.semaphore_signal(barrier, inc=1, device_id=dev, device_id_type=MESH)

    rows = pl.ds(pl.multiple_of(core * 32, 32), 32)

    def copy(index, qq, ss, l, dev):
        where = g.at[qq, ss, l, :, rows, :]
        return pltpu.make_async_remote_copy(
            src_ref=where, dst_ref=where, send_sem=send.at[index], recv_sem=recv.at[index],
            device_id=dev, device_id_type=MESH,
        )

    for load in loads:
        load.wait()
    st = stencil[0]
    st = jnp.concatenate([st, st], axis=1)

    def compute(l, faces):
        d = jnp.concatenate([deriv[f, 0] for f in faces], axis=0)
        values = jnp.dot(d, solve[l], preferred_element_type=F32)
        dd = [jnp.concatenate([diag[f]] * 4, axis=1) for f in faces]
        w = [cut[l, f].astype(F32) * coef[l, f] for f in faces]
        return leaf_rows(values, dd, st, w, faces, core, s, q)

    shared = (1 - s, 3 - q)
    x0, y1 = copy(0, q, s, 0, xdev), copy(1, q, s, 1, ydev)
    x1, y0 = copy(2, q, s, 1, xdev), copy(3, q, s, 0, ydev)
    c0, c1 = copy(4, q, s, 0, cdev), copy(5, q, s, 1, cdev)
    started = [x0, y1, c0, c1, x1, y0]
    for l in range(2):
        for t, tile in enumerate(compute(l, shared)):
            g[q, s, l, 0, rows, t * 128 : t * 128 + 128] = tile[:32]
            g[q, s, l, 1, rows, t * 128 : t * 128 + 128] = tile[32:]
        if l == 0:
            pl.semaphore_wait(barrier, 3)
            x0.start()
        else:
            y1.start()
            c0.start()
            c1.start()
    kept = (s, 2 + q, 4, 5)
    for l in range(2):
        for t, tile in enumerate(compute(l, kept)):
            own[l, :, t * 128 : t * 128 + 128] = tile
    stored = [pltpu.make_async_copy(own, own_out, leave.at[8])]
    stored[0].start()

    def store(index, qq, ss, l):
        one = pltpu.make_async_copy(g.at[qq, ss, l], g_out.at[qq, ss, l], leave.at[index])
        one.start()
        stored.append(one)

    x0.wait_send()
    x1.start()
    y1.wait_send()
    y0.start()
    later = [
        (x0, [(6, q, 1 - s, 0, ydev), (7, q, 1 - s, 0, cdev)]),
        (y1, [(8, 1 - q, s, 1, xdev), (9, 1 - q, s, 1, cdev)]),
        (x1, [(10, q, 1 - s, 1, cdev)]),
        (y0, [(11, 1 - q, s, 0, cdev)]),
    ]
    done = {}
    for first, relays in later:
        first.wait_recv()
        for relay in relays:
            done[relay[0]] = copy(*relay)
            done[relay[0]].start()
    c0.wait_recv()
    store(0, q, s, 0)
    c1.wait_recv()
    store(1, q, s, 1)
    done[7].wait_recv()
    store(2, q, 1 - s, 0)
    done[9].wait_recv()
    store(3, 1 - q, s, 1)
    done[10].wait_recv()
    store(4, q, 1 - s, 1)
    done[11].wait_recv()
    store(5, 1 - q, s, 0)
    done[6].wait_recv()
    done[12] = copy(12, 1 - q, 1 - s, 0, cdev)
    done[12].start()
    done[8].wait_recv()
    done[13] = copy(13, 1 - q, 1 - s, 1, cdev)
    done[13].start()
    done[12].wait_recv()
    store(6, 1 - q, 1 - s, 0)
    done[13].wait_recv()
    store(7, 1 - q, 1 - s, 1)
    for one in started[2:] + list(done.values()):
        one.wait_send()
    for one in stored:
        one.wait()


def split(x):
    hi = x.astype(BF16)
    return hi, (x - hi.astype(F32)).astype(BF16)


def dot(a, b):
    return jnp.dot(a, b, preferred_element_type=F32)


def mul(a, b):
    ah, al = split(a)
    bh, bl = split(b)
    both = jnp.concatenate([ah, al], axis=1)
    if b.shape[1] == 128:
        weights = jnp.concatenate(
            [jnp.concatenate([bh, bl], axis=1), jnp.concatenate([bh, jnp.zeros_like(bl)], axis=1)], axis=0
        )
        out = dot(both, weights)
        return out[:, :128] + out[:, 128:]
    return dot(both, jnp.concatenate([bh, bh], axis=0)) + dot(ah, bl)


def invert(mats, steps):
    row = lax.broadcasted_iota(jnp.int32, (128, 128), 0)
    eye = (row == lanes_of((128, 128))).astype(F32)
    state = []
    for m in mats:
        mt = m.T
        gram = mul(m, mt)
        scale = 1.9 / jnp.max(jnp.sum(jnp.abs(gram), axis=1, keepdims=True), axis=0, keepdims=True)
        state += [mt * scale, eye - gram * scale]

    def size(st):
        worst = jnp.maximum(jnp.abs(st[1]), jnp.abs(st[3]))
        return jnp.max(worst)

    def step(st):
        out = []
        for x, r in ((st[0], st[1]), (st[2], st[3])):
            both = mul(jnp.concatenate([x, r], axis=0), r)
            out += [x + both[:128], both[128:]]
        return out

    def body(carry):
        st = list(carry[2:])
        st = step(st)
        return (carry[0] + 1, size(st), *st)

    st = state
    for _ in range(steps):
        st = step(st)
    final = lax.while_loop(
        lambda c: jnp.logical_and(c[0] < LIMIT, c[1] > 1e-4), body, (jnp.int32(0), size(st), *st)
    )
    out = []
    for m, x in zip(mats, (final[2], final[4])):
        out.append(x + mul(x, eye - mul(m, x)))
    return out


def merge_kernel(g_in, own_in, result, out, sems, g, own, arrive):
    early = [
        pltpu.make_async_copy(
            g_in.at[:, :, :, 0, :, 256:384], g.at[:, :, :, 0, :, 256:384], arrive.at[0]
        )
    ]
    late = [
        pltpu.make_async_copy(g_in.at[:, :, :, 1], g.at[:, :, :, 1], arrive.at[1]),
        pltpu.make_async_copy(
            g_in.at[:, :, :, 0, :, 0:256], g.at[:, :, :, 0, :, 0:256], arrive.at[2]
        ),
        pltpu.make_async_copy(own_in, own, arrive.at[3]),
    ]
    early[0].start()
    early[0].wait()
    for load in late:
        load.start()
    me = lax.axis_index("leaf")
    s, q = me % 2, me // 2 % 2
    left64 = lanes_of((64, 128)) < 64
    left128 = lanes_of((128, 128)) < 64
    pairs = (q, 1 - q)
    zero = jnp.zeros((64, 128), F32)
    mats = []
    for p in pairs:
        sums = [g[p, 0, l, 0, :, 256:384] + g[p, 1, l, 0, :, 256:384] for l in range(2)]
        mats.append(
            jnp.concatenate(
                [jnp.where(left64, sums[0], zero), jnp.where(left64, zero, turn(sums[1]))], axis=0
            )
        )
    inverses = invert(mats, 8)
    for load in late:
        load.wait()
    weights = []
    for p, inverse, extra in zip(pairs, inverses, (True, False)):
        rows = [
            jnp.where(left64, g[p, e, 0, 1, :, 256:384], turn(g[p, e, 1, 1, :, 256:384])) for e in range(2)
        ]
        if extra:
            rows.append(jnp.where(left128, own[0, :, 256:384], turn(own[1, :, 256:384])))
        weights.append(mul(jnp.concatenate(rows, axis=0), inverse))

    schur, coupled, keep_outer, keep_inner = [], [], [], []
    for l in range(2):
        inner_tiles, outer_parts = [], []
        for p, w, extra in zip(pairs, weights, (True, False)):
            wl = w if l == 0 else turn(w)
            left = lanes_of(wl.shape) < 64
            hi = wl.astype(BF16).astype(F32)
            lo = wl - hi
            lhs = jnp.concatenate(
                [jnp.where(left, hi, turn(lo)).astype(BF16), jnp.where(left, hi, 0.0).astype(BF16)], axis=1
            )
            joint = jnp.where(left64, turn(g[p, 0, l, 0, :, 256:384]), g[p, 1, l, 0, :, 256:384])
            right = jnp.concatenate([g[p, 0, l, 0, :, 0:256], g[p, 1, l, 0, :, 0:256], joint], axis=1)
            bh, bl = split(right)
            prod = dot(lhs, jnp.concatenate([bh, bh, bl, bl], axis=0))
            zeros = jnp.zeros((64, 256), F32)
            base = jnp.concatenate(
                [
                    jnp.concatenate(
                        [
                            g[p, 0, l, 1, :, 0:256],
                            zeros,
                            jnp.where(left64, turn(g[p, 0, l, 1, :, 256:384]), zero),
                        ],
                        axis=1,
                    ),
                    jnp.concatenate(
                        [zeros, g[p, 1, l, 1, :, 0:256], jnp.where(left64, zero, g[p, 1, l, 1, :, 256:384])],
                        axis=1,
                    ),
                ],
                axis=0,
            )
            rows = base - prod[:128]
            outer_parts.append(rows[:, :512])
            inner_tiles.append(rows[:, 512:])
            if extra:
                first = s == 0
                mine = own[l, :, 0:256]
                face = own[l, :, 256:384]
                keep_outer.append(
                    jnp.concatenate([jnp.where(first, mine, 0.0), jnp.where(first, 0.0, mine)], axis=1)
                    - prod[128:, :512]
                )
                placed = jnp.where(
                    left128, jnp.where(first, turn(face), 0.0), jnp.where(first, 0.0, face)
                )
                keep_inner.append(placed - prod[128:, 512:])
        schur.append(inner_tiles[0] + inner_tiles[1])
        coupled.append(outer_parts)
    inverses = invert(schur, 9)
    here = pl.ds(pl.multiple_of(q * 512, 512), 512)
    there = pl.ds(pl.multiple_of((1 - q) * 512, 512), 512)
    copies = []
    for l in range(2):
        w = mul(keep_inner[l], inverses[l])
        for part, place in enumerate((here, there)):
            value = mul(w, coupled[l][part])
            out[2 * l + part] = keep_outer[l] - value if part == 0 else -value
            one = pltpu.make_async_copy(out.at[2 * l + part], result.at[l, :, place], sems.at[2 * l + part])
            one.start()
            copies.append(one)
    for one in copies:
        one.wait()


def local(solve_ops, inner_deriv, boundary_diag, wall_stencil, wall_coef, cut_faces):
    leaves, inner, bound = solve_ops.shape
    faces, _, half, _ = inner_deriv.shape
    hbm = pl.BlockSpec(memory_space=pltpu.HBM)
    arrays = (solve_ops, inner_deriv, boundary_diag, wall_stencil, wall_coef, cut_faces)
    g, own = pl.pallas_call(
        gather_kernel,
        out_shape=(
            jax.ShapeDtypeStruct((2, 2, leaves, 2, 2 * half, bound), F32),
            jax.ShapeDtypeStruct((leaves, 4 * half, bound), F32),
        ),
        in_specs=[hbm] * 6,
        out_specs=(hbm, hbm),
        scratch_shapes=[pltpu.SemaphoreType.DMA((14,)), pltpu.SemaphoreType.DMA((14,))]
        + [pltpu.VMEM(a.shape, a.dtype) for a in arrays[:4]]
        + [pltpu.SMEM(a.shape, a.dtype) for a in arrays[4:]]
        + [
            pltpu.SemaphoreType.DMA((6,)),
            pltpu.VMEM((2, 2, leaves, 2, 2 * half, bound), F32),
            pltpu.VMEM((leaves, 4 * half, bound), F32),
            pltpu.SemaphoreType.DMA((9,)),
        ],
        compiler_params=pltpu.CompilerParams(
            collective_id=0, has_side_effects=True, vmem_limit_bytes=60 * 1024 * 1024
        ),
        name="gather_rows",
    )(*arrays)
    merged = pl.pallas_call(
        merge_kernel,
        out_shape=jax.ShapeDtypeStruct((leaves, 4 * half, 16 * 2 * half), F32),
        in_specs=[hbm, hbm],
        out_specs=hbm,
        scratch_shapes=[
            pltpu.VMEM((2 * leaves, 4 * half, 8 * 2 * half), F32),
            pltpu.SemaphoreType.DMA((4,)),
            pltpu.VMEM(g.shape, F32),
            pltpu.VMEM(own.shape, F32),
            pltpu.SemaphoreType.DMA((4,)),
        ],
        compiler_params=pltpu.CompilerParams(vmem_limit_bytes=60 * 1024 * 1024),
        name="merge_levels",
    )(g, own)
    return merged.reshape(leaves, 4, 1, half, 16 * 2 * half)


def solution(mesh):
    in_specs = (
        P("leaf", None, None),
        P(None, "face", None, None),
        P(None, "face", None),
        P("face", None, None),
        P("leaf", None),
        P("leaf", None),
    )
    out_specs = P("leaf", None, "face", None, None)
    return jax.shard_map(local, mesh=mesh, in_specs=in_specs, out_specs=out_specs, check_vma=False)
```

```python
import functools

import jax
import jax.numpy as jnp
from jax import lax
from jax.experimental import pallas as pl
from jax.experimental.pallas import tpu as pltpu
from jax.sharding import PartitionSpec as P

MESH = pl.DeviceIdType.MESH
F32 = jnp.float32
BF16 = jnp.bfloat16
LIMIT = 60


def lanes_of(shape):
    return lax.broadcasted_iota(jnp.int32, shape, len(shape) - 1)


def turn(x):
    return pltpu.roll(x, 64, 1)


def leaf_rows(values, diag, stencil, weights, faces, core, s, q):
    half = 32
    lane = lanes_of((half, 128))
    row = lax.broadcasted_iota(jnp.int32, (half, 128), 0)
    tiles = []
    for n, face in enumerate(faces):
        part = values[n * half : (n + 1) * half]
        side = face % 2
        spot = lane - side * 64
        extra = jnp.where(spot == core * half + row, diag[n], 0.0)
        on = jnp.logical_and(spot >= 0, spot < 64)
        extra = extra + jnp.where(on, stencil * weights[n], 0.0)
        tiles.append(
            [part[:, t * 128 : t * 128 + 128] + jnp.where(face // 2 == t, extra, 0.0) for t in range(3)]
        )
    xt, yt, zt = (jnp.concatenate([row_tiles[t] for row_tiles in tiles], axis=0) for t in range(3))
    left = lanes_of(xt.shape) < 64
    xr, yr = turn(xt), turn(yt)
    first, lower = s == 0, q == 0
    outer = jnp.where(left, jnp.where(first, xt, xr), jnp.where(lower, yr, yt))
    inner = jnp.where(left, jnp.where(first, xr, xt), jnp.where(lower, yt, yr))
    return outer, zt, inner


def gather_kernel(*refs):
    sources, (g_out, own_out, send, recv), held, (arrive, g, own, leave) = (
        refs[:6], refs[6:10], refs[10:16], refs[16:]
    )
    solve, deriv, diag, stencil, coef, cut = held
    loads = [
        pltpu.make_async_copy(src, dst, arrive.at[n]) for n, (src, dst) in enumerate(zip(sources, held))
    ]
    for load in loads:
        load.start()
    me = lax.axis_index("leaf")
    core = lax.axis_index("face")
    s, q = me % 2, me // 2 % 2
    xdev = (me + 1 - 2 * s, core)
    ydev = (me + 2 - 4 * q, core)
    cdev = (me, 1 - core)
    barrier = pltpu.get_barrier_semaphore()
    for dev in (xdev, ydev, cdev):
        pl.semaphore_signal(barrier, inc=1, device_id=dev, device_id_type=MESH)

    rows = pl.ds(pl.multiple_of(core * 32, 32), 32)

    def copy(index, qq, ss, l, dev):
        where = g.at[qq, ss, l, :, rows, :]
        return pltpu.make_async_remote_copy(
            src_ref=where, dst_ref=where, send_sem=send.at[index], recv_sem=recv.at[index],
            device_id=dev, device_id_type=MESH,
        )

    for load in loads:
        load.wait()
    st = stencil[0]
    st = jnp.concatenate([st, st], axis=1)

    def compute(l, faces):
        d = jnp.concatenate([deriv[f, 0] for f in faces], axis=0)
        values = jnp.dot(d, solve[l], preferred_element_type=F32)
        dd = [jnp.concatenate([diag[f]] * 4, axis=1) for f in faces]
        w = [cut[l, f].astype(F32) * coef[l, f] for f in faces]
        return leaf_rows(values, dd, st, w, faces, core, s, q)

    shared = (1 - s, 3 - q)
    x0, y1 = copy(0, q, s, 0, xdev), copy(1, q, s, 1, ydev)
    x1, y0 = copy(2, q, s, 1, xdev), copy(3, q, s, 0, ydev)
    c0, c1 = copy(4, q, s, 0, cdev), copy(5, q, s, 1, cdev)
    started = [x0, y1, c0, c1, x1, y0]
    for l in range(2):
        for t, tile in enumerate(compute(l, shared)):
            g[q, s, l, 0, rows, t * 128 : t * 128 + 128] = tile[:32]
            g[q, s, l, 1, rows, t * 128 : t * 128 + 128] = tile[32:]
        if l == 0:
            pl.semaphore_wait(barrier, 3)
            x0.start()
        else:
            for one in started[1:]:
                one.start()
    kept = (s, 2 + q, 4, 5)
    for l in range(2):
        for t, tile in enumerate(compute(l, kept)):
            own[l, :, t * 128 : t * 128 + 128] = tile
    stored = [pltpu.make_async_copy(own, own_out, leave.at[8])]
    stored[0].start()

    def store(index, qq, ss, l):
        one = pltpu.make_async_copy(g.at[qq, ss, l], g_out.at[qq, ss, l], leave.at[index])
        one.start()
        stored.append(one)

    later = [
        (x0, [(6, q, 1 - s, 0, ydev), (7, q, 1 - s, 0, cdev)]),
        (y1, [(8, 1 - q, s, 1, xdev), (9, 1 - q, s, 1, cdev)]),
        (x1, [(10, q, 1 - s, 1, cdev)]),
        (y0, [(11, 1 - q, s, 0, cdev)]),
    ]
    done = {}
    for first, relays in later:
        first.wait_recv()
        for relay in relays:
            done[relay[0]] = copy(*relay)
            done[relay[0]].start()
    c0.wait_recv()
    store(0, q, s, 0)
    c1.wait_recv()
    store(1, q, s, 1)
    done[7].wait_recv()
    store(2, q, 1 - s, 0)
    done[9].wait_recv()
    store(3, 1 - q, s, 1)
    done[10].wait_recv()
    store(4, q, 1 - s, 1)
    done[11].wait_recv()
    store(5, 1 - q, s, 0)
    done[6].wait_recv()
    done[12] = copy(12, 1 - q, 1 - s, 0, cdev)
    done[12].start()
    done[8].wait_recv()
    done[13] = copy(13, 1 - q, 1 - s, 1, cdev)
    done[13].start()
    done[12].wait_recv()
    store(6, 1 - q, 1 - s, 0)
    done[13].wait_recv()
    store(7, 1 - q, 1 - s, 1)
    for one in started + list(done.values()):
        one.wait_send()
    for one in stored:
        one.wait()


def split(x):
    hi = x.astype(BF16)
    return hi, (x - hi.astype(F32)).astype(BF16)


def dot(a, b):
    return jnp.dot(a, b, preferred_element_type=F32)


def mul(a, b):
    ah, al = split(a)
    bh, bl = split(b)
    both = jnp.concatenate([ah, al], axis=1)
    if b.shape[1] == 128:
        weights = jnp.concatenate(
            [jnp.concatenate([bh, bl], axis=1), jnp.concatenate([bh, jnp.zeros_like(bl)], axis=1)], axis=0
        )
        out = dot(both, weights)
        return out[:, :128] + out[:, 128:]
    return dot(both, jnp.concatenate([bh, bh], axis=0)) + dot(ah, bl)


def invert(mats, steps):
    row = lax.broadcasted_iota(jnp.int32, (128, 128), 0)
    eye = (row == lanes_of((128, 128))).astype(F32)
    state = []
    for m in mats:
        mt = m.T
        gram = mul(m, mt)
        scale = 1.9 / jnp.max(jnp.sum(jnp.abs(gram), axis=1, keepdims=True), axis=0, keepdims=True)
        state += [mt * scale, eye - gram * scale]

    def size(st):
        worst = jnp.maximum(jnp.abs(st[1]), jnp.abs(st[3]))
        return jnp.max(worst)

    def step(st):
        out = []
        for x, r in ((st[0], st[1]), (st[2], st[3])):
            both = mul(jnp.concatenate([x, r], axis=0), r)
            out += [x + both[:128], both[128:]]
        return out

    def body(carry):
        st = list(carry[2:])
        st = step(st)
        return (carry[0] + 1, size(st), *st)

    st = state
    for _ in range(steps):
        st = step(st)
    final = lax.while_loop(
        lambda c: jnp.logical_and(c[0] < LIMIT, c[1] > 1e-4), body, (jnp.int32(0), size(st), *st)
    )
    out = []
    for m, x in zip(mats, (final[2], final[4])):
        out.append(x + mul(x, eye - mul(m, x)))
    return out


def merge_kernel(g_in, own_in, result, out, sems, g, own, arrive):
    early = [
        pltpu.make_async_copy(
            g_in.at[:, :, :, 0, :, 256:384], g.at[:, :, :, 0, :, 256:384], arrive.at[0]
        )
    ]
    late = [
        pltpu.make_async_copy(g_in.at[:, :, :, 1], g.at[:, :, :, 1], arrive.at[1]),
        pltpu.make_async_copy(
            g_in.at[:, :, :, 0, :, 0:256], g.at[:, :, :, 0, :, 0:256], arrive.at[2]
        ),
        pltpu.make_async_copy(own_in, own, arrive.at[3]),
    ]
    early[0].start()
    early[0].wait()
    for load in late:
        load.start()
    me = lax.axis_index("leaf")
    s, q = me % 2, me // 2 % 2
    left64 = lanes_of((64, 128)) < 64
    left128 = lanes_of((128, 128)) < 64
    pairs = (q, 1 - q)
    zero = jnp.zeros((64, 128), F32)
    mats = []
    for p in pairs:
        sums = [g[p, 0, l, 0, :, 256:384] + g[p, 1, l, 0, :, 256:384] for l in range(2)]
        mats.append(
            jnp.concatenate(
                [jnp.where(left64, sums[0], zero), jnp.where(left64, zero, turn(sums[1]))], axis=0
            )
        )
    inverses = invert(mats, 8)
    for load in late:
        load.wait()
    weights = []
    for p, inverse, extra in zip(pairs, inverses, (True, False)):
        rows = [
            jnp.where(left64, g[p, e, 0, 1, :, 256:384], turn(g[p, e, 1, 1, :, 256:384])) for e in range(2)
        ]
        if extra:
            rows.append(jnp.where(left128, own[0, :, 256:384], turn(own[1, :, 256:384])))
        weights.append(mul(jnp.concatenate(rows, axis=0), inverse))

    schur, coupled, keep_outer, keep_inner = [], [], [], []
    for l in range(2):
        inner_tiles, outer_parts = [], []
        for p, w, extra in zip(pairs, weights, (True, False)):
            wl = w if l == 0 else turn(w)
            left = lanes_of(wl.shape) < 64
            hi = wl.astype(BF16).astype(F32)
            lo = wl - hi
            lhs = jnp.concatenate(
                [jnp.where(left, hi, turn(lo)).astype(BF16), jnp.where(left, hi, 0.0).astype(BF16)], axis=1
            )
            joint = jnp.where(left64, turn(g[p, 0, l, 0, :, 256:384]), g[p, 1, l, 0, :, 256:384])
            right = jnp.concatenate([g[p, 0, l, 0, :, 0:256], g[p, 1, l, 0, :, 0:256], joint], axis=1)
            bh, bl = split(right)
            prod = dot(lhs, jnp.concatenate([bh, bh, bl, bl], axis=0))
            zeros = jnp.zeros((64, 256), F32)
            base = jnp.concatenate(
                [
                    jnp.concatenate(
                        [
                            g[p, 0, l, 1, :, 0:256],
                            zeros,
                            jnp.where(left64, turn(g[p, 0, l, 1, :, 256:384]), zero),
                        ],
                        axis=1,
                    ),
                    jnp.concatenate(
                        [zeros, g[p, 1, l, 1, :, 0:256], jnp.where(left64, zero, g[p, 1, l, 1, :, 256:384])],
                        axis=1,
                    ),
                ],
                axis=0,
            )
            rows = base - prod[:128]
            outer_parts.append(rows[:, :512])
            inner_tiles.append(rows[:, 512:])
            if extra:
                first = s == 0
                mine = own[l, :, 0:256]
                face = own[l, :, 256:384]
                keep_outer.append(
                    jnp.concatenate([jnp.where(first, mine, 0.0), jnp.where(first, 0.0, mine)], axis=1)
                    - prod[128:, :512]
                )
                placed = jnp.where(
                    left128, jnp.where(first, turn(face), 0.0), jnp.where(first, 0.0, face)
                )
                keep_inner.append(placed - prod[128:, 512:])
        schur.append(inner_tiles[0] + inner_tiles[1])
        coupled.append(outer_parts)
    inverses = invert(schur, 9)
    here = pl.ds(pl.multiple_of(q * 512, 512), 512)
    there = pl.ds(pl.multiple_of((1 - q) * 512, 512), 512)
    copies = []
    for l in range(2):
        w = mul(keep_inner[l], inverses[l])
        for part, place in enumerate((here, there)):
            value = mul(w, coupled[l][part])
            out[2 * l + part] = keep_outer[l] - value if part == 0 else -value
            one = pltpu.make_async_copy(out.at[2 * l + part], result.at[l, :, place], sems.at[2 * l + part])
            one.start()
            copies.append(one)
    for one in copies:
        one.wait()


def local(solve_ops, inner_deriv, boundary_diag, wall_stencil, wall_coef, cut_faces):
    leaves, inner, bound = solve_ops.shape
    faces, _, half, _ = inner_deriv.shape
    hbm = pl.BlockSpec(memory_space=pltpu.HBM)
    arrays = (solve_ops, inner_deriv, boundary_diag, wall_stencil, wall_coef, cut_faces)
    g, own = pl.pallas_call(
        gather_kernel,
        out_shape=(
            jax.ShapeDtypeStruct((2, 2, leaves, 2, 2 * half, bound), F32),
            jax.ShapeDtypeStruct((leaves, 4 * half, bound), F32),
        ),
        in_specs=[hbm] * 6,
        out_specs=(hbm, hbm),
        scratch_shapes=[pltpu.SemaphoreType.DMA((14,)), pltpu.SemaphoreType.DMA((14,))]
        + [pltpu.VMEM(a.shape, a.dtype) for a in arrays[:4]]
        + [pltpu.SMEM(a.shape, a.dtype) for a in arrays[4:]]
        + [
            pltpu.SemaphoreType.DMA((6,)),
            pltpu.VMEM((2, 2, leaves, 2, 2 * half, bound), F32),
            pltpu.VMEM((leaves, 4 * half, bound), F32),
            pltpu.SemaphoreType.DMA((9,)),
        ],
        compiler_params=pltpu.CompilerParams(
            collective_id=0, has_side_effects=True, vmem_limit_bytes=60 * 1024 * 1024
        ),
        name="gather_rows",
    )(*arrays)
    merged = pl.pallas_call(
        merge_kernel,
        out_shape=jax.ShapeDtypeStruct((leaves, 4 * half, 16 * 2 * half), F32),
        in_specs=[hbm, hbm],
        out_specs=hbm,
        scratch_shapes=[
            pltpu.VMEM((2 * leaves, 4 * half, 8 * 2 * half), F32),
            pltpu.SemaphoreType.DMA((4,)),
            pltpu.VMEM(g.shape, F32),
            pltpu.VMEM(own.shape, F32),
            pltpu.SemaphoreType.DMA((4,)),
        ],
        compiler_params=pltpu.CompilerParams(vmem_limit_bytes=60 * 1024 * 1024),
        name="merge_levels",
    )(g, own)
    return merged.reshape(leaves, 4, 1, half, 16 * 2 * half)


def solution(mesh):
    in_specs = (
        P("leaf", None, None),
        P(None, "face", None, None),
        P(None, "face", None),
        P("face", None, None),
        P("leaf", None),
        P("leaf", None),
    )
    out_specs = P("leaf", None, "face", None, None)
    return jax.shard_map(local, mesh=mesh, in_specs=in_specs, out_specs=out_specs, check_vma=False)
```

```python
import functools

import jax
import jax.numpy as jnp
from jax import lax
from jax.experimental import pallas as pl
from jax.experimental.pallas import tpu as pltpu
from jax.sharding import PartitionSpec as P

MESH = pl.DeviceIdType.MESH
F32 = jnp.float32
BF16 = jnp.bfloat16
LIMIT = 60


def lanes_of(shape):
    return lax.broadcasted_iota(jnp.int32, shape, len(shape) - 1)


def turn(x):
    return pltpu.roll(x, 64, 1)


def leaf_rows(values, diag, stencil, weights, faces, core, s, q):
    half = 32
    lane = lanes_of((half, 128))
    row = lax.broadcasted_iota(jnp.int32, (half, 128), 0)
    tiles = []
    for n, face in enumerate(faces):
        part = values[n * half : (n + 1) * half]
        side = face % 2
        spot = lane - side * 64
        extra = jnp.where(spot == core * half + row, diag[n], 0.0)
        on = jnp.logical_and(spot >= 0, spot < 64)
        extra = extra + jnp.where(on, stencil * weights[n], 0.0)
        tiles.append(
            [part[:, t * 128 : t * 128 + 128] + jnp.where(face // 2 == t, extra, 0.0) for t in range(3)]
        )
    xt, yt, zt = (jnp.concatenate([row_tiles[t] for row_tiles in tiles], axis=0) for t in range(3))
    left = lanes_of(xt.shape) < 64
    xr, yr = turn(xt), turn(yt)
    first, lower = s == 0, q == 0
    outer = jnp.where(left, jnp.where(first, xt, xr), jnp.where(lower, yr, yt))
    inner = jnp.where(left, jnp.where(first, xr, xt), jnp.where(lower, yt, yr))
    return outer, zt, inner


def gather_kernel(*refs):
    sources, (g_out, own_out, send, recv), held, (arrive, g, own, leave) = (
        refs[:6], refs[6:10], refs[10:16], refs[16:]
    )
    solve, deriv, diag, stencil, coef, cut = held
    loads = [
        pltpu.make_async_copy(src, dst, arrive.at[n]) for n, (src, dst) in enumerate(zip(sources, held))
    ]
    for load in loads:
        load.start()
    me = lax.axis_index("leaf")
    core = lax.axis_index("face")
    s, q = me % 2, me // 2 % 2
    xdev = (me + 1 - 2 * s, core)
    ydev = (me + 2 - 4 * q, core)
    cdev = (me, 1 - core)
    barrier = pltpu.get_barrier_semaphore()
    for dev in (xdev, ydev, cdev):
        pl.semaphore_signal(barrier, inc=1, device_id=dev, device_id_type=MESH)

    rows = pl.ds(pl.multiple_of(core * 32, 32), 32)

    def copy(index, qq, ss, l, dev):
        where = g.at[qq, ss, l, :, rows, :]
        return pltpu.make_async_remote_copy(
            src_ref=where, dst_ref=where, send_sem=send.at[index], recv_sem=recv.at[index],
            device_id=dev, device_id_type=MESH,
        )

    for load in loads:
        load.wait()
    st = stencil[0]
    st = jnp.concatenate([st, st], axis=1)

    def compute(l, faces):
        d = jnp.concatenate([deriv[f, 0] for f in faces], axis=0)
        values = jnp.dot(d, solve[l], preferred_element_type=F32)
        dd = [jnp.concatenate([diag[f]] * 4, axis=1) for f in faces]
        w = [cut[l, f].astype(F32) * coef[l, f] for f in faces]
        return leaf_rows(values, dd, st, w, faces, core, s, q)

    shared = (1 - s, 3 - q)
    x0, y1 = copy(0, q, s, 0, xdev), copy(1, q, s, 1, ydev)
    x1, y0 = copy(2, q, s, 1, xdev), copy(3, q, s, 0, ydev)
    c0, c1 = copy(4, q, s, 0, cdev), copy(5, q, s, 1, cdev)
    started = [x0, y1, c0, c1, x1, y0]
    for l in range(2):
        for t, tile in enumerate(compute(l, shared)):
            g[q, s, l, 0, rows, t * 128 : t * 128 + 128] = tile[:32]
            g[q, s, l, 1, rows, t * 128 : t * 128 + 128] = tile[32:]
        if l == 0:
            pl.semaphore_wait(barrier, 3)
            x0.start()
        else:
            y1.start()
            c0.start()
            c1.start()
    kept = (s, 2 + q, 4, 5)
    for l in range(2):
        for t, tile in enumerate(compute(l, kept)):
            own[l, :, t * 128 : t * 128 + 128] = tile
    stored = [pltpu.make_async_copy(own, own_out, leave.at[8])]
    stored[0].start()

    def store(index, qq, ss, l):
        one = pltpu.make_async_copy(g.at[qq, ss, l], g_out.at[qq, ss, l], leave.at[index])
        one.start()
        stored.append(one)

    x0.wait_send()
    x1.start()
    y1.wait_send()
    y0.start()
    later = [
        (x0, [(6, q, 1 - s, 0, ydev), (7, q, 1 - s, 0, cdev)]),
        (y1, [(8, 1 - q, s, 1, xdev), (9, 1 - q, s, 1, cdev)]),
        (x1, [(10, q, 1 - s, 1, cdev)]),
        (y0, [(11, 1 - q, s, 0, cdev)]),
    ]
    done = {}
    for first, relays in later:
        first.wait_recv()
        for relay in relays:
            done[relay[0]] = copy(*relay)
            done[relay[0]].start()
    c0.wait_recv()
    store(0, q, s, 0)
    c1.wait_recv()
    store(1, q, s, 1)
    done[7].wait_recv()
    store(2, q, 1 - s, 0)
    done[9].wait_recv()
    store(3, 1 - q, s, 1)
    done[10].wait_recv()
    store(4, q, 1 - s, 1)
    done[11].wait_recv()
    store(5, 1 - q, s, 0)
    done[6].wait_recv()
    done[12] = copy(12, 1 - q, 1 - s, 0, cdev)
    done[12].start()
    done[8].wait_recv()
    done[13] = copy(13, 1 - q, 1 - s, 1, cdev)
    done[13].start()
    done[12].wait_recv()
    store(6, 1 - q, 1 - s, 0)
    done[13].wait_recv()
    store(7, 1 - q, 1 - s, 1)
    for one in started[2:] + list(done.values()):
        one.wait_send()
    for one in stored:
        one.wait()


def split(x):
    hi = x.astype(BF16)
    return hi, (x - hi.astype(F32)).astype(BF16)


def dot(a, b):
    return jnp.dot(a, b, preferred_element_type=F32)


def mul(a, b):
    ah, al = split(a)
    bh, bl = split(b)
    both = jnp.concatenate([ah, al], axis=1)
    if b.shape[1] == 128:
        weights = jnp.concatenate(
            [jnp.concatenate([bh, bl], axis=1), jnp.concatenate([bh, jnp.zeros_like(bl)], axis=1)], axis=0
        )
        out = dot(both, weights)
        return out[:, :128] + out[:, 128:]
    return dot(both, jnp.concatenate([bh, bh], axis=0)) + dot(ah, bl)


def invert(mats, steps):
    row = lax.broadcasted_iota(jnp.int32, (128, 128), 0)
    eye = (row == lanes_of((128, 128))).astype(F32)
    state = []
    for m in mats:
        mt = m.T
        gram = mul(m, mt)
        scale = 1.9 / jnp.max(jnp.sum(jnp.abs(gram), axis=1, keepdims=True), axis=0, keepdims=True)
        state += [mt * scale, eye - gram * scale]

    def size(st):
        worst = jnp.maximum(jnp.abs(st[1]), jnp.abs(st[3]))
        return jnp.max(worst)

    def step(st):
        out = []
        for x, r in ((st[0], st[1]), (st[2], st[3])):
            both = mul(jnp.concatenate([x, r], axis=0), r)
            out += [x + both[:128], both[128:]]
        return out

    def body(carry):
        st = list(carry[2:])
        st = step(st)
        return (carry[0] + 1, size(st), *st)

    st = state
    for _ in range(steps):
        st = step(st)
    final = lax.while_loop(
        lambda c: jnp.logical_and(c[0] < LIMIT, c[1] > 1e-4), body, (jnp.int32(0), size(st), *st)
    )
    out = []
    for m, x in zip(mats, (final[2], final[4])):
        out.append(x + mul(x, eye - mul(m, x)))
    return out


def merge_kernel(g_in, own_in, result, out, sems, g, own, arrive):
    early = [
        pltpu.make_async_copy(
            g_in.at[:, :, :, 0, :, 256:384], g.at[:, :, :, 0, :, 256:384], arrive.at[0]
        )
    ]
    late = [
        pltpu.make_async_copy(g_in.at[:, :, :, 1], g.at[:, :, :, 1], arrive.at[1]),
        pltpu.make_async_copy(
            g_in.at[:, :, :, 0, :, 0:256], g.at[:, :, :, 0, :, 0:256], arrive.at[2]
        ),
        pltpu.make_async_copy(own_in, own, arrive.at[3]),
    ]
    early[0].start()
    early[0].wait()
    for load in late:
        load.start()
    me = lax.axis_index("leaf")
    s, q = me % 2, me // 2 % 2
    left64 = lanes_of((64, 128)) < 64
    left128 = lanes_of((128, 128)) < 64
    pairs = (q, 1 - q)
    zero = jnp.zeros((64, 128), F32)
    mats = []
    for p in pairs:
        sums = [g[p, 0, l, 0, :, 256:384] + g[p, 1, l, 0, :, 256:384] for l in range(2)]
        mats.append(
            jnp.concatenate(
                [jnp.where(left64, sums[0], zero), jnp.where(left64, zero, turn(sums[1]))], axis=0
            )
        )
    inverses = invert(mats, 7)
    for load in late:
        load.wait()
    weights = []
    for p, inverse, extra in zip(pairs, inverses, (True, False)):
        rows = [
            jnp.where(left64, g[p, e, 0, 1, :, 256:384], turn(g[p, e, 1, 1, :, 256:384])) for e in range(2)
        ]
        if extra:
            rows.append(jnp.where(left128, own[0, :, 256:384], turn(own[1, :, 256:384])))
        weights.append(mul(jnp.concatenate(rows, axis=0), inverse))

    schur, coupled, keep_outer, keep_inner = [], [], [], []
    for l in range(2):
        inner_tiles, outer_parts = [], []
        for p, w, extra in zip(pairs, weights, (True, False)):
            wl = w if l == 0 else turn(w)
            left = lanes_of(wl.shape) < 64
            hi = wl.astype(BF16).astype(F32)
            lo = wl - hi
            lhs = jnp.concatenate(
                [jnp.where(left, hi, turn(lo)).astype(BF16), jnp.where(left, hi, 0.0).astype(BF16)], axis=1
            )
            joint = jnp.where(left64, turn(g[p, 0, l, 0, :, 256:384]), g[p, 1, l, 0, :, 256:384])
            right = jnp.concatenate([g[p, 0, l, 0, :, 0:256], g[p, 1, l, 0, :, 0:256], joint], axis=1)
            bh, bl = split(right)
            prod = dot(lhs, jnp.concatenate([bh, bh, bl, bl], axis=0))
            zeros = jnp.zeros((64, 256), F32)
            base = jnp.concatenate(
                [
                    jnp.concatenate(
                        [
                            g[p, 0, l, 1, :, 0:256],
                            zeros,
                            jnp.where(left64, turn(g[p, 0, l, 1, :, 256:384]), zero),
                        ],
                        axis=1,
                    ),
                    jnp.concatenate(
                        [zeros, g[p, 1, l, 1, :, 0:256], jnp.where(left64, zero, g[p, 1, l, 1, :, 256:384])],
                        axis=1,
                    ),
                ],
                axis=0,
            )
            rows = base - prod[:128]
            outer_parts.append(rows[:, :512])
            inner_tiles.append(rows[:, 512:])
            if extra:
                first = s == 0
                mine = own[l, :, 0:256]
                face = own[l, :, 256:384]
                keep_outer.append(
                    jnp.concatenate([jnp.where(first, mine, 0.0), jnp.where(first, 0.0, mine)], axis=1)
                    - prod[128:, :512]
                )
                placed = jnp.where(
                    left128, jnp.where(first, turn(face), 0.0), jnp.where(first, 0.0, face)
                )
                keep_inner.append(placed - prod[128:, 512:])
        schur.append(inner_tiles[0] + inner_tiles[1])
        coupled.append(outer_parts)
    inverses = invert(schur, 8)
    here = pl.ds(pl.multiple_of(q * 512, 512), 512)
    there = pl.ds(pl.multiple_of((1 - q) * 512, 512), 512)
    copies = []
    for l in range(2):
        w = mul(keep_inner[l], inverses[l])
        for part, place in enumerate((here, there)):
            value = mul(w, coupled[l][part])
            out[2 * l + part] = keep_outer[l] - value if part == 0 else -value
            one = pltpu.make_async_copy(out.at[2 * l + part], result.at[l, :, place], sems.at[2 * l + part])
            one.start()
            copies.append(one)
    for one in copies:
        one.wait()


def local(solve_ops, inner_deriv, boundary_diag, wall_stencil, wall_coef, cut_faces):
    leaves, inner, bound = solve_ops.shape
    faces, _, half, _ = inner_deriv.shape
    hbm = pl.BlockSpec(memory_space=pltpu.HBM)
    arrays = (solve_ops, inner_deriv, boundary_diag, wall_stencil, wall_coef, cut_faces)
    g, own = pl.pallas_call(
        gather_kernel,
        out_shape=(
            jax.ShapeDtypeStruct((2, 2, leaves, 2, 2 * half, bound), F32),
            jax.ShapeDtypeStruct((leaves, 4 * half, bound), F32),
        ),
        in_specs=[hbm] * 6,
        out_specs=(hbm, hbm),
        scratch_shapes=[pltpu.SemaphoreType.DMA((14,)), pltpu.SemaphoreType.DMA((14,))]
        + [pltpu.VMEM(a.shape, a.dtype) for a in arrays[:4]]
        + [pltpu.SMEM(a.shape, a.dtype) for a in arrays[4:]]
        + [
            pltpu.SemaphoreType.DMA((6,)),
            pltpu.VMEM((2, 2, leaves, 2, 2 * half, bound), F32),
            pltpu.VMEM((leaves, 4 * half, bound), F32),
            pltpu.SemaphoreType.DMA((9,)),
        ],
        compiler_params=pltpu.CompilerParams(
            collective_id=0, has_side_effects=True, vmem_limit_bytes=60 * 1024 * 1024
        ),
        name="gather_rows",
    )(*arrays)
    merged = pl.pallas_call(
        merge_kernel,
        out_shape=jax.ShapeDtypeStruct((leaves, 4 * half, 16 * 2 * half), F32),
        in_specs=[hbm, hbm],
        out_specs=hbm,
        scratch_shapes=[
            pltpu.VMEM((2 * leaves, 4 * half, 8 * 2 * half), F32),
            pltpu.SemaphoreType.DMA((4,)),
            pltpu.VMEM(g.shape, F32),
            pltpu.VMEM(own.shape, F32),
            pltpu.SemaphoreType.DMA((4,)),
        ],
        compiler_params=pltpu.CompilerParams(vmem_limit_bytes=60 * 1024 * 1024),
        name="merge_levels",
    )(g, own)
    return merged.reshape(leaves, 4, 1, half, 16 * 2 * half)


def solution(mesh):
    in_specs = (
        P("leaf", None, None),
        P(None, "face", None, None),
        P(None, "face", None),
        P("face", None, None),
        P("leaf", None),
        P("leaf", None),
    )
    out_specs = P("leaf", None, "face", None, None)
    return jax.shard_map(local, mesh=mesh, in_specs=in_specs, out_specs=out_specs, check_vma=False)
```
